512 devices in a mesh: cell: 64 (over z, y), view: 8 (over x, core).
Axes of the slice: x: 4, y: 4, z: 16, core: 2. Of those that a mesh axis runs over, the one named last changes fastest.
Arguments:
- params: float32 [7, 524288], P(None, 'cell'), may hold values from -4.5 to 4.5
- first_moment: float32 [7, 524288], P(None, 'cell'), may hold values from -6e-05 to 6e-05
- second_moment: float32 [7, 524288], P(None, 'cell'), may hold values from 1e-11 to 1e-08
- camera: float32 [1, 8, 4], P(None, 'view'), may hold values from -0.3 to 0.3
- slot_block: int32 [1, 8, 64, 64, 2], P(None, 'view', 'cell'), may hold values from -1 to 63, as said below
- slot_anchor: float32 [1, 8, 64, 2, 64, 2], P(None, 'view', 'cell'), may hold values from -0.3 to 0.3
- tile_items: int32 [1, 8, 512, 4], P(None, 'view', 'cell'), may hold values from 0 to 127, as said below
- target: float32 [1, 8, 512, 3, 256], P(None, 'view', 'cell'), may hold values from 0 to 1
Outputs:
- new_params: float32 [7, 524288], P(None, 'cell')
- tile_loss: float32 [1, 8, 512], P(None, 'view', 'cell')
The draws below stay inside these ranges and needn't reach their ends.
Inputs may be any that keep to these rules, and one draw needn't show every extreme that they name: `slot_block`: -1 marks an empty slot; in every step and view each owner receives all 2 slots from some cell. `tile_items`: entry c * 2 + j names the live slot j from cell c to the tile's owner (tile // 8); every live slot is named exactly once, and the 4 entries of a tile come from distinct cells.
All inputs are finite; a program needn't handle non-finite values.
Results may differ from the reference program's by a relative error of at most 0.00035.
Values sent between devices are 32-bit elements; how exact they have to be, the bound alone decides.
A program may use at most 64 MiB of HBM per device.

```python
import math
import jax
import jax.numpy as jnp
import numpy as np
from jax import lax

SIDE = 16
PIX = 256
BLOCK = 128
PARAMS = 7
TAPS = 11
DEPTH = 4
STEPS = 1
TILE_DEV = 8
BLOCKS_DEV = 64
CAP = 2
VIEWS = 8
TILES = 512
GAUSS = 524288
N_CELL = 64


def routing_tables(key):
    base_key = jax.random.fold_in(key, 7177)
    number_of_slots = N_CELL * CAP
    item_count = TILE_DEV * DEPTH

    def one_view(view_key):
        heat_key, rest_key = jax.random.split(view_key)
        warmth_level = jax.random.randint(heat_key, (N_CELL,), 0, 8) ** 2

        def one_owner(owner_key):
            sub_keys = jax.random.split(owner_key, 5)
            warmest_entry = jax.random.randint(sub_keys[0], (), 0, N_CELL)
            extra_warmth = jnp.where(jnp.arange(N_CELL) == warmest_entry, 1000, 0)
            source_items = jnp.arange(number_of_slots) // CAP
            random_noise = jax.random.randint(sub_keys[1], (number_of_slots,), 0, 4096)
            score_values = ((warmth_level + extra_warmth)[source_items] * 1024 + random_noise) * number_of_slots + jnp.arange(number_of_slots)
            unused_values, chosen = lax.top_k(score_values, item_count)
            chosen = jnp.sort(chosen)
            columns = chosen.reshape(DEPTH, TILE_DEV).T
            depth_keys = jax.random.split(sub_keys[2], TILE_DEV)
            orders = jax.vmap(lambda row_key: jax.random.permutation(row_key, DEPTH))(depth_keys)
            columns = jnp.take_along_axis(columns, orders, axis=1)
            tile_order = jax.random.permutation(sub_keys[3], TILE_DEV)
            columns = columns[tile_order]
            used_flags = jnp.zeros((number_of_slots,), jnp.int32).at[chosen].set(1)
            block_ids = jax.random.randint(sub_keys[4], (number_of_slots,), 0, BLOCKS_DEV)
            slot_table = jnp.where(used_flags > 0, block_ids, -1).reshape(N_CELL, CAP)
            return (slot_table, columns)
        owner_keys = jax.random.split(rest_key, N_CELL)
        slot_table, columns = jax.vmap(one_owner)(owner_keys)
        return (jnp.transpose(slot_table, (1, 0, 2)), columns.reshape(N_CELL * TILE_DEV, DEPTH))
    view_keys = jax.random.split(base_key, STEPS * VIEWS)
    slot_table, columns = jax.vmap(one_view)(view_keys)
    return (slot_table.reshape(STEPS, VIEWS, N_CELL, N_CELL, CAP), columns.reshape(STEPS, VIEWS, TILES, DEPTH))


def draw_slot_block(key, part):
    return routing_tables(key)[0].astype(jnp.int32)


def draw_tile_items(key, part):
    return routing_tables(key)[1].astype(jnp.int32)


def draw_params(key, part):
    sub_keys = jax.random.split(jax.random.fold_in(key, 31), 4)
    count = GAUSS
    place_xy = jax.random.uniform(sub_keys[0], (2, count), jnp.float32, 0.0, 1.0)
    log_scale = jax.random.uniform(sub_keys[1], (1, count), jnp.float32, -3.0, -1.6)
    opacity_logit = jnp.clip(1.5 * jax.random.normal(sub_keys[2], (1, count), jnp.float32), -4.5, 4.5)
    colour_logit = jnp.clip(1.5 * jax.random.normal(sub_keys[3], (3, count), jnp.float32), -4.5, 4.5)
    return jnp.concatenate([place_xy, log_scale, opacity_logit, colour_logit], axis=0)


def steps_of(rng, extent, cuts, low, top_value):
    def one(position, shards_of):
        heights = jax.random.uniform(jax.random.fold_in(jax.random.fold_in(rng, 6), position), (shards_of,), jnp.float32, low / len(cuts), top_value / len(cuts))
        return jnp.repeat(jnp.exp(heights), extent[position] // shards_of).reshape((-1,) + (1,) * (len(extent) - position - 1))

    gain = one(*cuts[0])
    for cut in cuts[1:]:
        gain = gain * one(*cut)
    return gain


def bell_draw(key, shape, deviation, reach, cuts=(), held_as=jnp.bfloat16):
    array = deviation * jax.random.normal(key, shape, jnp.float32)
    if cuts:
        array = array * steps_of(key, shape, cuts, -0.22, 0.18)
    return jnp.clip(array, -reach, reach).astype(held_as)


def setup_inputs(seed: int = 0) -> dict:
    streams_of = jax.random.split(jax.random.key(seed), 9)
    params = draw_params(jax.random.fold_in(streams_of[8], 71), 0)
    first_moment = bell_draw(streams_of[1], (PARAMS, GAUSS), 0.00001, 5.999999848427251e-05, ((1, 64),), jnp.float32)
    second_moment = jnp.clip(jnp.exp(math.log(9.99999993922529e-09) - 6.9077553 * jax.random.uniform(streams_of[2], (PARAMS, GAUSS), jnp.float32) ** steps_of(streams_of[2], (PARAMS, GAUSS), ((1, 64),), -0.2, 0.2)), 9.999999960041972e-12, 9.99999993922529e-09)
    camera = jnp.clip(jax.random.uniform(streams_of[3], (STEPS, VIEWS, 4), jnp.float32, -0.3, 0.3) * steps_of(streams_of[3], (STEPS, VIEWS, 4), ((1, 8),), -0.4, 0.0), -0.3, 0.3)
    slot_block = draw_slot_block(jax.random.fold_in(streams_of[8], 71), 0)
    slot_anchor = jnp.clip(jax.random.uniform(streams_of[5], (STEPS, VIEWS, N_CELL, 2, N_CELL, CAP), jnp.float32, -0.3, 0.3) * steps_of(streams_of[5], (STEPS, VIEWS, N_CELL, 2, N_CELL, CAP), ((1, 8), (2, 64)), -0.4, 0.0), -0.3, 0.3)
    tile_items = draw_tile_items(jax.random.fold_in(streams_of[8], 71), 0)
    target = jnp.clip(1.0 * jax.random.uniform(streams_of[7], (STEPS, VIEWS, TILES, 3, PIX), jnp.float32) ** steps_of(streams_of[7], (STEPS, VIEWS, TILES, 3, PIX), ((1, 8), (2, 64)), -0.2, 0.2), 0.0, 1.0)
    return dict(params=params, first_moment=first_moment, second_moment=second_moment, camera=camera, slot_block=slot_block, slot_anchor=slot_anchor, tile_items=tile_items, target=target)


ssim_weight = 0.2
stable_one = 0.0001
stable_two = 0.0009
learn_rate = 0.1
beta_one = 0.9
beta_two = 0.999
adam_eps = 1e-08
first_step = 1
opacity_cap = 0.1
weight_floor = 0.5
highest = lax.Precision.HIGHEST

def blur_matrix(tile_side, taps_count):
    offsets = np.arange(tile_side)[:, None] - np.arange(tile_side)[None, :]
    kernel = np.exp(-(offsets * offsets) / 4.5) * (np.abs(offsets) <= taps_count // 2)
    kernel = kernel / kernel.sum(axis=1, keepdims=True)
    return jnp.asarray(np.kron(kernel, kernel).T, jnp.float32)

def pixel_grid(tile_side):
    places = jnp.arange(tile_side * tile_side, dtype=jnp.int32)
    grid_x = ((places % tile_side).astype(jnp.float32) + 0.5) / tile_side
    grid_y = ((places // tile_side).astype(jnp.float32) + 0.5) / tile_side
    return (grid_x, grid_y)

def splat_block(block_params, camera_row, anchors, grid_x, grid_y):
    pos_x = block_params[:, 0]
    pos_y = block_params[:, 1]
    mean_u = (1.0 + camera_row[0]) * pos_x + camera_row[1] * pos_y + anchors[:, 0:1]
    mean_w = camera_row[2] * pos_x + (1.0 + camera_row[3]) * pos_y + anchors[:, 1:2]
    inverse = 0.5 * jnp.exp(-2.0 * block_params[:, 2])
    opacity = opacity_cap * jax.nn.sigmoid(block_params[:, 3])
    colours = jax.nn.sigmoid(block_params[:, 4:7])
    delta_x = grid_x[None, None, :] - mean_u[:, :, None]
    delta_y = grid_y[None, None, :] - mean_w[:, :, None]
    alphas = opacity[:, :, None] * jnp.exp(-(delta_x * delta_x + delta_y * delta_y) * inverse[:, :, None])
    weighted = jnp.einsum('ncg,ngp->ncp', colours, alphas, precision=highest)
    totals = lax.optimization_barrier(jnp.sum(alphas, axis=1))
    transmit = jnp.exp(lax.optimization_barrier(jnp.sum(jnp.log1p(-alphas), axis=1)))
    shaded = (1.0 - transmit)[:, None, :] * weighted / jnp.maximum(totals, weight_floor)[:, None, :]
    return jnp.concatenate([shaded, transmit[:, None, :]], axis=1)

def merge_tiles(items):
    fronts = jnp.ones_like(items[:, 0, 3])
    images = jnp.zeros_like(items[:, 0, :3])
    for rank_index in range(items.shape[1]):
        images = images + fronts[:, None, :] * items[:, rank_index, :3]
        fronts = fronts * items[:, rank_index, 3]
    return images

def tile_losses(images, goal_tiles, blur_table):
    tile_count = images.shape[0]
    predicted = images.reshape(tile_count * 3, -1)
    wanted = goal_tiles.reshape(tile_count * 3, -1)
    stacked = jnp.concatenate([predicted, wanted, predicted * predicted, wanted * wanted, predicted * wanted], axis=0)
    blurred = jnp.dot(stacked, blur_table, precision=highest, preferred_element_type=jnp.float32)
    local_pred, local_goal, square_pred, square_goal, cross_term = jnp.split(blurred, 5, axis=0)
    var_pred = square_pred - local_pred * local_pred
    var_goal = square_goal - local_goal * local_goal
    cov_both = cross_term - local_pred * local_goal
    similar = (2.0 * local_pred * local_goal + stable_one) * (2.0 * cov_both + stable_two) / ((local_pred * local_pred + local_goal * local_goal + stable_one) * (var_pred + var_goal + stable_two))
    residue = predicted - wanted
    values = (1.0 - ssim_weight) * residue * residue + ssim_weight * (1.0 - similar)
    return lax.optimization_barrier(jnp.mean(values.reshape(tile_count, -1), axis=1))

def reference(params, first_moment, second_moment, camera, slot_block, slot_anchor, tile_items, target):
    blur_table = blur_matrix(SIDE, TAPS)
    grid_x, grid_y = pixel_grid(SIDE)
    per_cell = BLOCKS_DEV * BLOCK
    lane_ids = jnp.arange(BLOCK, dtype=jnp.int32)
    owners = jnp.arange(N_CELL, dtype=jnp.int32)
    current = params
    moment_one = first_moment
    moment_two = second_moment
    loss_rows = []
    for step_index in range(STEPS):

        def view_step(summed, view_data):
            camera_row, blocks_view, anchors_view, items_view, goals_view = view_data

            def owner_pass(gradient, owner_id):
                entries = lax.dynamic_slice_in_dim(items_view, owner_id * TILE_DEV, TILE_DEV, 0).reshape(-1)
                source_items = entries // CAP
                slot_id = entries % CAP
                block_id = blocks_view[source_items, owner_id, slot_id]
                anchors = anchors_view[source_items, :, owner_id, slot_id]
                gauss_index = (source_items * per_cell + block_id * BLOCK)[:, None] + lane_ids[None, :]
                item_params = jnp.transpose(current[:, gauss_index], (1, 0, 2))
                goal_tiles = lax.dynamic_slice_in_dim(goals_view, owner_id * TILE_DEV, TILE_DEV, 0)

                def owner_loss(inner_params):
                    partial_value = splat_block(inner_params, camera_row, anchors, grid_x, grid_y)
                    return tile_losses(merge_tiles(partial_value.reshape(TILE_DEV, DEPTH, 4, PIX)), goal_tiles, blur_table)
                losses, pullback = jax.vjp(owner_loss, item_params)
                item_grads = pullback(jnp.ones_like(losses))[0]
                gradient = gradient.at[:, gauss_index].add(jnp.transpose(item_grads, (1, 0, 2)))
                return (gradient, losses)
            gradient, losses = lax.scan(owner_pass, jnp.zeros_like(current), owners)
            return (summed + gradient, losses.reshape(-1))
        gradient, losses = lax.scan(view_step, jnp.zeros_like(current), (camera[step_index], slot_block[step_index], slot_anchor[step_index], tile_items[step_index], target[step_index]))
        loss_rows.append(losses)
        step_count = first_step + step_index
        fix_one = 1.0 - beta_one ** step_count
        fix_two = 1.0 - beta_two ** step_count
        moment_one = beta_one * moment_one + (1.0 - beta_one) * gradient
        moment_two = beta_two * moment_two + (1.0 - beta_two) * gradient * gradient
        current = current - learn_rate * (moment_one / fix_one) / (jnp.sqrt(moment_two / fix_two) + adam_eps)
    return (current, jnp.stack(loss_rows))
```

```python
import functools

import jax
import jax.numpy as jnp
import numpy as np
from jax import lax
from jax.experimental import pallas as pl
from jax.experimental.pallas import tpu as pltpu
from jax.sharding import PartitionSpec as P

SIDE = 16
PIX = 256
BLOCK = 128
COMP = 7
TAPS = 11
DEPTH = 4
TILES = 8
NCELL = 64
NVIEW = 8
NBLOCK = 64
CAP = 2
NZ = 16
NY = 4
GROUP = 8

SSIM_WEIGHT = 0.2
STABLE_ONE = 0.0001
STABLE_TWO = 0.0009
LEARN_RATE = 0.1
BETA_ONE = 0.9
BETA_TWO = 0.999
ADAM_EPS = 1e-08
FIRST_STEP = 1
OPACITY_CAP = 0.1
WEIGHT_FLOOR = 0.5

F32 = jnp.float32
MESH = pl.DeviceIdType.MESH
HIGHEST = lax.Precision.HIGHEST


def blur_matrix():
    offsets = np.arange(SIDE)[:, None] - np.arange(SIDE)[None, :]
    kernel = np.exp(-(offsets * offsets) / 4.5) * (np.abs(offsets) <= TAPS // 2)
    kernel = kernel / kernel.sum(axis=1, keepdims=True)
    return jnp.asarray(np.kron(kernel, kernel).T, F32)


def cell_peer(i, z, y):
    k = lax.div(i, NY)
    m = lax.div(k + 1, 2)
    dz = jnp.where(lax.rem(k, 2) == 1, m, NZ - m)
    return lax.rem(z + dz, NZ) * NY + lax.rem(y + i, NY)


def send_blocks(camera_ref, ids_ref, anchor_ref, params_ref, out_ref, derived, tx, send_sem, recv_sem):
    c = lax.axis_index("cell")
    v = lax.axis_index("view")
    z, y = lax.div(c, NY), lax.rem(c, NY)
    barrier = pltpu.get_barrier_semaphore()

    @pl.loop(1, NCELL, unroll=9)
    def _(i):
        pl.semaphore_signal(
            barrier, inc=1, device_id=(cell_peer(i, z, y), v), device_id_type=MESH
        )

    q0, q1, q2, q3 = (camera_ref[0, i] for i in range(4))
    width = 1024
    for part in range(NBLOCK * BLOCK // width):
        lanes = pl.ds(part * width, width)
        values = params_ref[:, lanes]
        row = lax.broadcasted_iota(jnp.int32, values.shape, 0)
        logistic = 1.0 / (1.0 + jnp.exp(-values))
        inverse = 0.5 * jnp.exp(-2.0 * values)
        pos_x, pos_y = values[0:1], values[1:2]
        base_u = (1.0 + q0) * pos_x + q1 * pos_y
        base_w = q2 * pos_x + (1.0 + q3) * pos_y
        out = jnp.where(row == 3, OPACITY_CAP * logistic, logistic)
        out = jnp.where(row == 2, inverse, out)
        out = jnp.where(row == 1, base_w, out)
        out = jnp.where(row == 0, base_u, out)
        for i in range(width // BLOCK):
            derived[1 + part * (width // BLOCK) + i] = out[:, i * BLOCK : (i + 1) * BLOCK]
    derived[0] = jnp.zeros((COMP, BLOCK), F32)

    pl.semaphore_wait(barrier, NCELL - 1)

    def gather(o):
        row = lax.broadcasted_iota(jnp.int32, (COMP, BLOCK), 0)
        for j in range(CAP):
            tile = derived[ids_ref[j, o] + 1]
            shift = jnp.where(
                row == 0, anchor_ref[j, o], jnp.where(row == 1, anchor_ref[CAP + j, o], 0.0)
            )
            tx[o, j] = tile + shift

    @pl.loop(1, NCELL, unroll=3)
    def _(i):
        o = cell_peer(i, z, y)
        gather(o)
        pltpu.make_async_remote_copy(
            src_ref=tx.at[o],
            dst_ref=out_ref.at[c],
            send_sem=send_sem,
            recv_sem=recv_sem,
            device_id=(o, v),
            device_id_type=MESH,
        ).start()

    gather(c)
    pltpu.make_async_copy(tx.at[c], out_ref.at[c], recv_sem).start()
    pltpu.make_async_copy(tx, out_ref, recv_sem).wait()
    rest = pl.ds(0, NCELL - 1)
    pltpu.make_async_copy(tx.at[rest], out_ref.at[rest], send_sem).wait()


def render(camera_ref, items_ref, rx_ref, goal_ref, blur_ref, grad_ref, loss_ref, alphas, merged, back):
    lane = lax.broadcasted_iota(jnp.int32, (GROUP, 128), 1)
    level = lax.broadcasted_iota(jnp.int32, (GROUP, 128), 0)
    grid_x = ((lane & (SIDE - 1)).astype(F32) + 0.5) / SIDE
    grid_y = [((lane >> 4).astype(F32) + (0.5 + half * 8)) / SIDE for half in range(2)]
    halves = [pl.ds(0, 128), pl.ds(128, 128)]

    def columns(e):
        tile = rx_ref[e >> 1, e & 1]
        return tile, jnp.transpose(jnp.concatenate([tile, jnp.zeros((1, BLOCK), F32)], axis=0))

    def spread(cols, g, i):
        return jnp.broadcast_to(cols[g * GROUP : (g + 1) * GROUP, i : i + 1], (GROUP, 128))

    @pl.loop(0, TILES)
    def _(t):
        for k in range(DEPTH):
            _, cols = columns(items_ref[k, t])
            slot = t * DEPTH + k
            clear = [jnp.ones((GROUP, 128), F32) for _ in range(2)]
            sums = [[jnp.zeros((GROUP, 128), F32) for _ in range(4)] for _ in range(2)]
            for g in range(BLOCK // GROUP):
                u, w, inverse, opacity, c0, c1, c2 = (spread(cols, g, i) for i in range(COMP))
                dx = grid_x - u
                dx2 = dx * dx
                for half in range(2):
                    dy = grid_y[half] - w
                    alpha = opacity * jnp.exp(-(dx2 + dy * dy) * inverse)
                    alphas[slot, pl.ds(g * GROUP, GROUP), halves[half]] = alpha
                    clear[half] = clear[half] * (1.0 - alpha)
                    s = sums[half]
                    s[0] = s[0] + alpha
                    s[1] = s[1] + c0 * alpha
                    s[2] = s[2] + c1 * alpha
                    s[3] = s[3] + c2 * alpha
            for half in range(2):
                p = clear[half]
                for step in (4, 2, 1):
                    p = p * pltpu.roll(p, step, 0)
                for i, whole in enumerate([p, *sums[half]]):
                    if i:
                        whole = jnp.sum(whole, axis=0, keepdims=True)
                    merged[i, k, :, halves[half]] = jnp.where(
                        level == t, whole, merged[i, k, :, halves[half]]
                    )

    fronts = [jnp.ones((TILES, PIX), F32)]
    images = [jnp.zeros((TILES, PIX), F32) for _ in range(3)]
    colours = []
    for k in range(DEPTH):
        transmit, total = merged[0, k], merged[1, k]
        scale = (1.0 - transmit) / jnp.maximum(total, WEIGHT_FLOOR)
        shaded = [scale * merged[2 + ch, k] for ch in range(3)]
        images = [images[ch] + fronts[k] * shaded[ch] for ch in range(3)]
        colours.append(shaded)
        fronts.append(fronts[k] * transmit)

    a = jnp.concatenate(images, axis=0)
    b = jnp.concatenate([goal_ref[ch] for ch in range(3)], axis=0)
    rows = 3 * TILES
    blurred = jnp.dot(
        jnp.concatenate([a, b, a * a, b * b, a * b], axis=0),
        blur_ref[...],
        precision=HIGHEST,
        preferred_element_type=F32,
    )
    ma, mb, saa, sbb, sab = (blurred[i * rows : (i + 1) * rows] for i in range(5))
    va = saa - ma * ma
    vb = sbb - mb * mb
    cab = sab - ma * mb
    n1 = 2.0 * ma * mb + STABLE_ONE
    n2 = 2.0 * cab + STABLE_TWO
    d1 = ma * ma + mb * mb + STABLE_ONE
    d2 = va + vb + STABLE_TWO
    under = 1.0 / (d1 * d2)
    ssim = n1 * n2 * under
    apart = a - b
    values = (1.0 - SSIM_WEIGHT) * apart * apart + SSIM_WEIGHT * (1.0 - ssim)
    per_tile = values[0:TILES] + values[TILES : 2 * TILES] + values[2 * TILES :]
    count = 3.0 * PIX
    loss = jnp.sum(per_tile, axis=1, keepdims=True) / count
    sub = lax.broadcasted_iota(jnp.int32, (TILES, TILES), 0)
    col = lax.broadcasted_iota(jnp.int32, (TILES, TILES), 1)
    loss_ref[...] = jnp.sum(jnp.where(sub == col, loss, 0.0), axis=0, keepdims=True)

    g_s = -SSIM_WEIGHT / count
    g_n1 = g_s * n2 * under
    g_n2 = g_s * n1 * under
    g_d1 = -g_s * ssim / d1
    g_d2 = -g_s * ssim / d2
    g_ab = 2.0 * g_n2
    g_ma = 2.0 * mb * g_n1 + 2.0 * ma * g_d1 - mb * g_ab - 2.0 * ma * g_d2
    backed = lax.dot_general(
        jnp.concatenate([g_ma, g_d2, g_ab], axis=0),
        blur_ref[...],
        (((1,), (1,)), ((), ())),
        precision=HIGHEST,
        preferred_element_type=F32,
    )
    g_image = (
        (2.0 * (1.0 - SSIM_WEIGHT) / count) * apart
        + backed[0:rows]
        + 2.0 * a * backed[rows : 2 * rows]
        + b * backed[2 * rows :]
    )
    g_ch = [g_image[ch * TILES : (ch + 1) * TILES] for ch in range(3)]
    g_front = jnp.zeros((TILES, PIX), F32)
    for k in reversed(range(DEPTH)):
        transmit, total = merged[0, k], merged[1, k]
        floor = jnp.maximum(total, WEIGHT_FLOOR)
        over = 1.0 / floor
        shade = (1.0 - transmit) * over
        lit = sum(g_ch[ch] * merged[2 + ch, k] for ch in range(3)) * over * fronts[k]
        g_transmit = fronts[k] * g_front - lit
        share = jnp.where(total > WEIGHT_FLOOR, 1.0, jnp.where(total == WEIGHT_FLOOR, 0.5, 0.0))
        ways = [fronts[k] * g_ch[ch] * shade for ch in range(3)]
        for i, way in enumerate([*ways, -share * lit * shade, g_transmit * transmit]):
            for half in range(2):
                back[i, k, half] = way[:, half * 128 : (half + 1) * 128]
        g_front = sum(g_ch[ch] * colours[k][ch] for ch in range(3)) + transmit * g_front

    @pl.loop(0, NCELL)
    def _(i):
        grad_ref[i] = jnp.zeros((CAP, COMP, BLOCK), F32)

    q0, q1, q2, q3 = (camera_ref[0, i] for i in range(4))

    @pl.loop(0, TILES)
    def _(t):
        for k in range(DEPTH):
            e = items_ref[k, t]
            tile, cols = columns(e)
            slot = t * DEPTH + k
            rays = [
                [
                    jnp.broadcast_to(back[i, k, half, pl.ds(t, 1), :], (GROUP, 128))
                    for half in range(2)
                ]
                for i in range(5)
            ]
            pieces = []
            for g in range(BLOCK // GROUP):
                u, w, _, _, c0, c1, c2 = (spread(cols, g, i) for i in range(COMP))
                dx = grid_x - u
                q_sum = qy = qr = None
                tints = [None] * 3
                for half in range(2):
                    alpha = alphas[slot, pl.ds(g * GROUP, GROUP), halves[half]]
                    dy = grid_y[half] - w
                    slope = (
                        c0 * rays[0][half]
                        + c1 * rays[1][half]
                        + c2 * rays[2][half]
                        + rays[3][half]
                        - rays[4][half] / (1.0 - alpha)
                    )
                    q = slope * alpha
                    qd = q * dy
                    parts = [q, qd, qd * dy] + [rays[ch][half] * alpha for ch in range(3)]
                    if half == 0:
                        q_sum, qy, qr, *tints = parts
                    else:
                        q_sum, qy, qr = q_sum + parts[0], qy + parts[1], qr + parts[2]
                        tints = [tints[ch] + parts[3 + ch] for ch in range(3)]
                qx = q_sum * dx
                qr = qr + qx * dx
                lane8 = lax.broadcasted_iota(jnp.int32, (GROUP, GROUP), 1)
                piece = jnp.zeros((GROUP, GROUP), F32)
                for i, value in enumerate([qx, qy, qr, q_sum, *tints]):
                    piece = jnp.where(lane8 == i, jnp.sum(value, axis=1, keepdims=True), piece)
                pieces.append(piece)
            sums = jnp.transpose(jnp.concatenate(pieces, axis=0))
            twice = 2.0 * tile[2:3]
            du = twice * sums[0:1]
            dw = twice * sums[1:2]
            tone = tile[4:7]
            grad_ref[e >> 1, e & 1] = jnp.concatenate(
                [
                    (1.0 + q0) * du + q2 * dw,
                    q1 * du + (1.0 + q3) * dw,
                    twice * sums[2:3],
                    (1.0 - tile[3:4] / OPACITY_CAP) * sums[3:4],
                    tone * (1.0 - tone) * sums[4:7],
                ],
                axis=0,
            )


def return_and_step(
    grad_ref, ids_ref, params_ref, first_ref, second_ref, out_ref,
    rx, spread, shares, rows, mine, send_sem, recv_sem, part_send, part_recv, row_send, row_recv,
):
    c = lax.axis_index("cell")
    v = lax.axis_index("view")
    z, y = lax.div(c, NY), lax.rem(c, NY)
    barrier = pltpu.get_barrier_semaphore()

    @pl.loop(1, NCELL, unroll=9)
    def _(i):
        pl.semaphore_signal(
            barrier, inc=1, device_id=(cell_peer(i, z, y), v), device_id_type=MESH
        )

    for i in range(1, NVIEW):
        pl.semaphore_signal(
            barrier, inc=1, device_id=(c, lax.rem(v + i, NVIEW)), device_id_type=MESH
        )
    pl.semaphore_wait(barrier, NCELL - 1 + NVIEW - 1)

    @pl.loop(1, NCELL, unroll=3)
    def _(i):
        o = cell_peer(i, z, y)
        pltpu.make_async_remote_copy(
            src_ref=grad_ref.at[o],
            dst_ref=rx.at[c],
            send_sem=send_sem,
            recv_sem=recv_sem,
            device_id=(o, v),
            device_id_type=MESH,
        ).start()

    pltpu.make_async_copy(grad_ref.at[c], rx.at[c], recv_sem).start()

    ids = jnp.concatenate([ids_ref[0:1, :], ids_ref[1:2, :]], axis=1)
    block = lax.broadcasted_iota(jnp.int32, (NBLOCK, CAP * NCELL), 0)
    chosen = jnp.where(block == ids, 1.0, 0.0).astype(F32)
    row = jnp.minimum(v, COMP - 1)
    level = lax.broadcasted_iota(jnp.int32, (COMP, BLOCK), 0)
    for b in range(NBLOCK):
        lanes = pl.ds(b * BLOCK, BLOCK)
        for i, ref in enumerate((params_ref, first_ref, second_ref)):
            only = jnp.where(level == row, ref[:, lanes], 0.0)
            mine[i, pl.ds(b, 1), :] = jnp.sum(only, axis=0, keepdims=True)

    pltpu.make_async_copy(grad_ref, rx, recv_sem).wait()

    for p in range(COMP):
        values = jnp.concatenate([rx[:, j, p, :] for j in range(CAP)], axis=0)
        spread[p] = jnp.dot(chosen, values, precision=HIGHEST, preferred_element_type=F32)

    def part(i):
        w = lax.rem(v + i, NVIEW)
        return w, pltpu.make_async_remote_copy(
            src_ref=spread.at[jnp.minimum(w, COMP - 1)],
            dst_ref=shares.at[v],
            send_sem=part_send.at[i],
            recv_sem=part_recv.at[v],
            device_id=(c, w),
            device_id_type=MESH,
        )

    def arrived(buffer, sem, s):
        return pltpu.make_async_copy(buffer.at[s], buffer.at[s], sem.at[s])

    for i in range(1, NVIEW):
        w, copy = part(i)
        pl.when(w < COMP)(copy.start)

    def send_row(i):
        return pltpu.make_async_remote_copy(
            src_ref=rows.at[row],
            dst_ref=rows.at[row],
            send_sem=row_send.at[i],
            recv_sem=row_recv.at[row],
            device_id=(c, lax.rem(v + i, NVIEW)),
            device_id_type=MESH,
        )

    @pl.when(v < COMP)
    def _():
        for s in range(NVIEW):
            pl.when(v != s)(arrived(shares, part_recv, s).wait)
        shares[v] = spread[row]
        grad = shares[0]
        for s in range(1, NVIEW):
            grad = grad + shares[s]
        one = BETA_ONE * mine[1] + (1.0 - BETA_ONE) * grad
        two = BETA_TWO * mine[2] + (1.0 - BETA_TWO) * grad * grad
        fix_one = 1.0 - BETA_ONE**FIRST_STEP
        fix_two = 1.0 - BETA_TWO**FIRST_STEP
        rows[row] = mine[0] - LEARN_RATE * (one / fix_one) / (jnp.sqrt(two / fix_two) + ADAM_EPS)
        for i in range(1, NVIEW):
            send_row(i).start()

    for p in range(COMP):
        pl.when(v != p)(arrived(rows, row_recv, p).wait)
        for b in range(NBLOCK):
            out_ref[pl.ds(p, 1), pl.ds(b * BLOCK, BLOCK)] = rows[p, pl.ds(b, 1), :]

    rest = pl.ds(0, NCELL - 1)
    pltpu.make_async_copy(grad_ref.at[rest], rx.at[rest], send_sem).wait()
    for i in range(1, NVIEW):
        w, copy = part(i)
        pl.when(w < COMP)(copy.wait_send)

    @pl.when(v < COMP)
    def _():
        for i in range(1, NVIEW):
            send_row(i).wait_send()


def shards(
    params, first_moment, second_moment, camera, slot_block, slot_anchor, tile_items, target
):
    vmem = pl.BlockSpec(memory_space=pltpu.VMEM)
    smem = pl.BlockSpec(memory_space=pltpu.SMEM)
    ids = jnp.transpose(slot_block[0, 0, 0], (1, 0))
    anchors = jnp.transpose(slot_anchor[0, 0, 0], (0, 2, 1)).reshape(2 * CAP, NCELL)
    items = jnp.transpose(tile_items[0, 0], (1, 0))
    goals = jnp.transpose(target[0, 0], (1, 0, 2))
    message = (NCELL, CAP, COMP, BLOCK)
    dma = pltpu.SemaphoreType.DMA
    arrived = pl.pallas_call(
        send_blocks,
        out_shape=jax.ShapeDtypeStruct(message, F32),
        in_specs=[smem, smem, smem, vmem],
        out_specs=vmem,
        scratch_shapes=[
            pltpu.VMEM((1 + NBLOCK, COMP, BLOCK), F32),
            pltpu.VMEM(message, F32),
            dma,
            dma,
        ],
        compiler_params=pltpu.CompilerParams(
            collective_id=0, has_side_effects=True, vmem_limit_bytes=24 << 20
        ),
    )(camera[0], ids, anchors, params)
    item_grads, losses = pl.pallas_call(
        render,
        out_shape=[
            jax.ShapeDtypeStruct(message, F32),
            jax.ShapeDtypeStruct((1, TILES), F32),
        ],
        in_specs=[smem, smem, vmem, vmem, vmem],
        out_specs=[vmem, vmem],
        scratch_shapes=[
            pltpu.VMEM((TILES * DEPTH, BLOCK, PIX), F32),
            pltpu.VMEM((5, DEPTH, TILES, PIX), F32),
            pltpu.VMEM((5, DEPTH, 2, TILES, 128), F32),
        ],
        compiler_params=pltpu.CompilerParams(vmem_limit_bytes=24 << 20),
    )(camera[0], items, arrived, goals, blur_matrix())
    share = (NVIEW, NBLOCK, BLOCK)
    new_params = pl.pallas_call(
        return_and_step,
        out_shape=jax.ShapeDtypeStruct((COMP, NBLOCK * BLOCK), F32),
        in_specs=[vmem] * 5,
        out_specs=vmem,
        scratch_shapes=[
            pltpu.VMEM(message, F32),
            pltpu.VMEM((COMP, NBLOCK, BLOCK), F32),
            pltpu.VMEM(share, F32),
            pltpu.VMEM((COMP, NBLOCK, BLOCK), F32),
            pltpu.VMEM((3, NBLOCK, BLOCK), F32),
            dma,
            dma,
            dma((NVIEW,)),
            dma((NVIEW,)),
            dma((NVIEW,)),
            dma((NVIEW,)),
        ],
        compiler_params=pltpu.CompilerParams(
            collective_id=1, has_side_effects=True, vmem_limit_bytes=24 << 20
        ),
    )(item_grads, ids, params, first_moment, second_moment)
    return (new_params, losses.reshape(1, 1, TILES))


def solution(mesh):
    placed = (
        P(None, "cell"),
        P(None, "cell"),
        P(None, "cell"),
        P(None, "view", None),
        P(None, "view", "cell", None, None),
        P(None, "view", "cell", None, None, None),
        P(None, "view", "cell", None),
        P(None, "view", "cell", None, None),
    )
    return jax.shard_map(
        shards,
        mesh=mesh,
        in_specs=placed,
        out_specs=(P(None, "cell"), P(None, "view", "cell")),
        check_vma=False,
    )
```

```python
import functools

import jax
import jax.numpy as jnp
import numpy as np
from jax import lax
from jax.experimental import pallas as pl
from jax.experimental.pallas import tpu as pltpu
from jax.sharding import PartitionSpec as P

SIDE = 16
PIX = 256
BLOCK = 128
COMP = 7
TAPS = 11
DEPTH = 4
TILES = 8
NCELL = 64
NVIEW = 8
NBLOCK = 64
CAP = 2
NZ = 16
NY = 4
GROUP = 8

SSIM_WEIGHT = 0.2
STABLE_ONE = 0.0001
STABLE_TWO = 0.0009
LEARN_RATE = 0.1
BETA_ONE = 0.9
BETA_TWO = 0.999
ADAM_EPS = 1e-08
FIRST_STEP = 1
OPACITY_CAP = 0.1
WEIGHT_FLOOR = 0.5

F32 = jnp.float32
MESH = pl.DeviceIdType.MESH
HIGHEST = lax.Precision.HIGHEST


def blur_matrix():
    offsets = np.arange(SIDE)[:, None] - np.arange(SIDE)[None, :]
    kernel = np.exp(-(offsets * offsets) / 4.5) * (np.abs(offsets) <= TAPS // 2)
    kernel = kernel / kernel.sum(axis=1, keepdims=True)
    return jnp.asarray(np.kron(kernel, kernel).T, F32)


def cell_peer(i, z, y):
    k = lax.div(i, NY)
    m = lax.div(k + 1, 2)
    dz = jnp.where(lax.rem(k, 2) == 1, m, NZ - m)
    return lax.rem(z + dz, NZ) * NY + lax.rem(y + i, NY)


def send_blocks(camera_ref, ids_ref, anchor_ref, params_ref, out_ref, derived, tx, send_sem, recv_sem):
    c = lax.axis_index("cell")
    v = lax.axis_index("view")
    z, y = lax.div(c, NY), lax.rem(c, NY)
    barrier = pltpu.get_barrier_semaphore()

    @pl.loop(1, NCELL, unroll=9)
    def _(i):
        pl.semaphore_signal(
            barrier, inc=1, device_id=(cell_peer(i, z, y), v), device_id_type=MESH
        )

    q0, q1, q2, q3 = (camera_ref[0, i] for i in range(4))
    width = 1024
    for part in range(NBLOCK * BLOCK // width):
        lanes = pl.ds(part * width, width)
        values = params_ref[:, lanes]
        row = lax.broadcasted_iota(jnp.int32, values.shape, 0)
        logistic = 1.0 / (1.0 + jnp.exp(-values))
        inverse = 0.5 * jnp.exp(-2.0 * values)
        pos_x, pos_y = values[0:1], values[1:2]
        base_u = (1.0 + q0) * pos_x + q1 * pos_y
        base_w = q2 * pos_x + (1.0 + q3) * pos_y
        out = jnp.where(row == 3, OPACITY_CAP * logistic, logistic)
        out = jnp.where(row == 2, inverse, out)
        out = jnp.where(row == 1, base_w, out)
        out = jnp.where(row == 0, base_u, out)
        for i in range(width // BLOCK):
            derived[1 + part * (width // BLOCK) + i] = out[:, i * BLOCK : (i + 1) * BLOCK]
    derived[0] = jnp.zeros((COMP, BLOCK), F32)

    pl.semaphore_wait(barrier, NCELL - 1)

    def gather(o):
        row = lax.broadcasted_iota(jnp.int32, (COMP, BLOCK), 0)
        for j in range(CAP):
            tile = derived[ids_ref[j, o] + 1]
            shift = jnp.where(
                row == 0, anchor_ref[j, o], jnp.where(row == 1, anchor_ref[CAP + j, o], 0.0)
            )
            tx[o, j] = tile + shift

    @pl.loop(1, NCELL, unroll=3)
    def _(i):
        o = cell_peer(i, z, y)
        gather(o)
        pltpu.make_async_remote_copy(
            src_ref=tx.at[o],
            dst_ref=out_ref.at[c],
            send_sem=send_sem,
            recv_sem=recv_sem,
            device_id=(o, v),
            device_id_type=MESH,
        ).start()

    gather(c)
    pltpu.make_async_copy(tx.at[c], out_ref.at[c], recv_sem).start()
    pltpu.make_async_copy(tx, out_ref, recv_sem).wait()
    rest = pl.ds(0, NCELL - 1)
    pltpu.make_async_copy(tx.at[rest], out_ref.at[rest], send_sem).wait()


def render(camera_ref, items_ref, rx_ref, goal_ref, blur_ref, grad_ref, loss_ref, alphas, merged, back):
    lane = lax.broadcasted_iota(jnp.int32, (GROUP, 128), 1)
    level = lax.broadcasted_iota(jnp.int32, (GROUP, 128), 0)
    grid_x = ((lane & (SIDE - 1)).astype(F32) + 0.5) / SIDE
    grid_y = [((lane >> 4).astype(F32) + (0.5 + half * 8)) / SIDE for half in range(2)]
    halves = [pl.ds(0, 128), pl.ds(128, 128)]

    def split(x, narrow=False):
        parts = []
        for _ in range(3):
            part = x.astype(jnp.bfloat16)
            parts.append(part if narrow else part.astype(F32))
            x = x - part.astype(F32)
        return parts

    def tinted(tile):
        shifted = jnp.concatenate([tile[4:7], tile[0:5]], axis=0)
        return jnp.where(level == 3, 1.0, jnp.where(level < 3, shifted, 0.0))

    level256 = lax.broadcasted_iota(jnp.int32, (GROUP, PIX), 0)

    def columns(e):
        tile = rx_ref[e >> 1, e & 1]
        return tile, jnp.transpose(jnp.concatenate([tile, jnp.zeros((1, BLOCK), F32)], axis=0))

    def spread(cols, g, i):
        return jnp.broadcast_to(cols[g * GROUP : (g + 1) * GROUP, i : i + 1], (GROUP, 128))

    @pl.loop(0, TILES)
    def _(t):
        for k in range(DEPTH):
            tile, cols = columns(items_ref[k, t])
            slot = t * DEPTH + k
            clear = [jnp.ones((GROUP, 128), F32) for _ in range(2)]
            for g in range(BLOCK // GROUP):
                u, w, inverse, opacity = (spread(cols, g, i) for i in range(4))
                dx = grid_x - u
                dx2 = dx * dx
                for half in range(2):
                    dy = grid_y[half] - w
                    alpha = opacity * jnp.exp(-(dx2 + dy * dy) * inverse)
                    alphas[slot, pl.ds(g * GROUP, GROUP), halves[half]] = alpha
                    clear[half] = clear[half] * (1.0 - alpha)
            alpha = alphas[slot]
            first = alpha.astype(jnp.bfloat16)
            second = (alpha - first.astype(F32)).astype(jnp.bfloat16)
            wh, wm, _ = split(tinted(tile))
            both = jnp.dot(jnp.concatenate([wh, wm], axis=0).astype(jnp.bfloat16), first, preferred_element_type=F32)
            rest = jnp.dot(jnp.concatenate([wh, wh], axis=0).astype(jnp.bfloat16), second, preferred_element_type=F32)
            sums = both[0:8] + both[8:16] + rest[0:8]
            for half in range(2):
                p = clear[half]
                for step in (4, 2, 1):
                    p = p * pltpu.roll(p, step, 0)
                merged[0, k, :, halves[half]] = jnp.where(level == t, p, merged[0, k, :, halves[half]])
            for i in range(4):
                merged[1 + i, k] = jnp.where(level256 == t, sums[3 if i == 0 else i - 1 : 4 if i == 0 else i], merged[1 + i, k])

    fronts = [jnp.ones((TILES, PIX), F32)]
    images = [jnp.zeros((TILES, PIX), F32) for _ in range(3)]
    colours = []
    for k in range(DEPTH):
        transmit, total = merged[0, k], merged[1, k]
        scale = (1.0 - transmit) / jnp.maximum(total, WEIGHT_FLOOR)
        shaded = [scale * merged[2 + ch, k] for ch in range(3)]
        images = [images[ch] + fronts[k] * shaded[ch] for ch in range(3)]
        colours.append(shaded)
        fronts.append(fronts[k] * transmit)

    a = jnp.concatenate(images, axis=0)
    b = jnp.concatenate([goal_ref[ch] for ch in range(3)], axis=0)
    rows = 3 * TILES
    blurred = jnp.dot(
        jnp.concatenate([a, b, a * a, b * b, a * b], axis=0),
        blur_ref[...],
        precision=HIGHEST,
        preferred_element_type=F32,
    )
    ma, mb, saa, sbb, sab = (blurred[i * rows : (i + 1) * rows] for i in range(5))
    va = saa - ma * ma
    vb = sbb - mb * mb
    cab = sab - ma * mb
    n1 = 2.0 * ma * mb + STABLE_ONE
    n2 = 2.0 * cab + STABLE_TWO
    d1 = ma * ma + mb * mb + STABLE_ONE
    d2 = va + vb + STABLE_TWO
    under = 1.0 / (d1 * d2)
    ssim = n1 * n2 * under
    apart = a - b
    values = (1.0 - SSIM_WEIGHT) * apart * apart + SSIM_WEIGHT * (1.0 - ssim)
    per_tile = values[0:TILES] + values[TILES : 2 * TILES] + values[2 * TILES :]
    count = 3.0 * PIX
    loss = jnp.sum(per_tile, axis=1, keepdims=True) / count
    sub = lax.broadcasted_iota(jnp.int32, (TILES, TILES), 0)
    col = lax.broadcasted_iota(jnp.int32, (TILES, TILES), 1)
    loss_ref[...] = jnp.sum(jnp.where(sub == col, loss, 0.0), axis=0, keepdims=True)

    g_s = -SSIM_WEIGHT / count
    g_n1 = g_s * n2 * under
    g_n2 = g_s * n1 * under
    g_d1 = -g_s * ssim / d1
    g_d2 = -g_s * ssim / d2
    g_ab = 2.0 * g_n2
    g_ma = 2.0 * mb * g_n1 + 2.0 * ma * g_d1 - mb * g_ab - 2.0 * ma * g_d2
    backed = lax.dot_general(
        jnp.concatenate([g_ma, g_d2, g_ab], axis=0),
        blur_ref[...],
        (((1,), (1,)), ((), ())),
        precision=HIGHEST,
        preferred_element_type=F32,
    )
    g_image = (
        (2.0 * (1.0 - SSIM_WEIGHT) / count) * apart
        + backed[0:rows]
        + 2.0 * a * backed[rows : 2 * rows]
        + b * backed[2 * rows :]
    )
    g_ch = [g_image[ch * TILES : (ch + 1) * TILES] for ch in range(3)]
    g_front = jnp.zeros((TILES, PIX), F32)
    back[...] = jnp.zeros((TILES, DEPTH, 8, PIX), F32)
    for k in reversed(range(DEPTH)):
        transmit, total = merged[0, k], merged[1, k]
        floor = jnp.maximum(total, WEIGHT_FLOOR)
        over = 1.0 / floor
        shade = (1.0 - transmit) * over
        lit = sum(g_ch[ch] * merged[2 + ch, k] for ch in range(3)) * over * fronts[k]
        g_transmit = fronts[k] * g_front - lit
        share = jnp.where(total > WEIGHT_FLOOR, 1.0, jnp.where(total == WEIGHT_FLOOR, 0.5, 0.0))
        ways = [fronts[k] * g_ch[ch] * shade for ch in range(3)]
        for i, way in enumerate([*ways, -share * lit * shade, g_transmit * transmit]):
            for at in range(TILES):
                back[at, k, i : i + 1, :] = way[at : at + 1]
        g_front = sum(g_ch[ch] * colours[k][ch] for ch in range(3)) + transmit * g_front

    def turned(rows, x):
        return lax.dot_general(rows, x, (((1,), (1,)), ((), ())), preferred_element_type=F32)

    def newton(x):
        r = pl.reciprocal(x, approx=True)
        return r * (2.0 - x * r)

    place = lax.broadcasted_iota(jnp.int32, (16, PIX), 1)
    kind = lax.broadcasted_iota(jnp.int32, (16, PIX), 0)
    at_x = ((place & (SIDE - 1)).astype(F32) - 7.5) / SIDE
    at_y = ((place >> 4).astype(F32) - 7.5) / SIDE
    basis = jnp.where(kind == 0, 1.0, jnp.where(kind == 1, at_x, jnp.where(kind == 2, at_y, jnp.where(kind == 3, at_x * at_x + at_y * at_y, 0.0)))).astype(jnp.bfloat16)

    @pl.loop(0, NCELL)
    def _(i):
        grad_ref[i] = jnp.zeros((CAP, COMP, BLOCK), F32)

    q0, q1, q2, q3 = (camera_ref[0, i] for i in range(4))

    @pl.loop(0, TILES)
    def _(t):
        for k in range(DEPTH):
            e = items_ref[k, t]
            tile = rx_ref[e >> 1, e & 1]
            slot = t * DEPTH + k
            rays = back[t, k]
            alpha = alphas[slot]
            ah, am, al = split(tinted(tile))
            rh, rm, rl = split(rays)
            slope = lax.dot_general(
                jnp.concatenate([ah, ah, am, am, ah, al], axis=0).astype(jnp.bfloat16),
                jnp.concatenate([rh, rm, rh, rm, rl, rh], axis=0).astype(jnp.bfloat16),
                (((0,), (0,)), ((), ())), preferred_element_type=F32)
            clear = 1.0 - alpha
            inv = newton(clear)
            q = (slope - rays[4:5] * inv) * alpha
            moments = sum(turned(basis, part) for part in split(q, True))
            first = alpha.astype(jnp.bfloat16)
            second = (alpha - first.astype(F32)).astype(jnp.bfloat16)
            both = turned(jnp.concatenate([rh, rm], axis=0).astype(jnp.bfloat16), first)
            tints = both[0:3] + both[8:11] + turned(jnp.concatenate([rh, rh], axis=0).astype(jnp.bfloat16), second)[0:3]
            m0, mx, my, mr = (moments[i:i+1] for i in range(4))
            cu, cw = tile[0:1] - 0.5, tile[1:2] - 0.5
            sums = jnp.concatenate([mx - cu * m0, my - cw * m0, mr - 2.0 * (cu * mx + cw * my) + (cu * cu + cw * cw) * m0, m0, tints], axis=0)
            twice = 2.0 * tile[2:3]
            du = twice * sums[0:1]
            dw = twice * sums[1:2]
            tone = tile[4:7]
            grad_ref[e >> 1, e & 1] = jnp.concatenate(
                [
                    (1.0 + q0) * du + q2 * dw,
                    q1 * du + (1.0 + q3) * dw,
                    twice * sums[2:3],
                    (1.0 - tile[3:4] / OPACITY_CAP) * sums[3:4],
                    tone * (1.0 - tone) * sums[4:7],
                ],
                axis=0,
            )


def return_and_step(
    grad_ref, ids_ref, params_ref, first_ref, second_ref, out_ref,
    rx, spread, shares, rows, mine, send_sem, recv_sem, part_send, part_recv, row_send, row_recv,
):
    c = lax.axis_index("cell")
    v = lax.axis_index("view")
    z, y = lax.div(c, NY), lax.rem(c, NY)
    barrier = pltpu.get_barrier_semaphore()

    @pl.loop(1, NCELL, unroll=9)
    def _(i):
        pl.semaphore_signal(
            barrier, inc=1, device_id=(cell_peer(i, z, y), v), device_id_type=MESH
        )

    for i in range(1, NVIEW):
        pl.semaphore_signal(
            barrier, inc=1, device_id=(c, lax.rem(v + i, NVIEW)), device_id_type=MESH
        )
    pl.semaphore_wait(barrier, NCELL - 1 + NVIEW - 1)

    @pl.loop(1, NCELL, unroll=3)
    def _(i):
        o = cell_peer(i, z, y)
        pltpu.make_async_remote_copy(
            src_ref=grad_ref.at[o],
            dst_ref=rx.at[c],
            send_sem=send_sem,
            recv_sem=recv_sem,
            device_id=(o, v),
            device_id_type=MESH,
        ).start()

    pltpu.make_async_copy(grad_ref.at[c], rx.at[c], recv_sem).start()

    ids = jnp.concatenate([ids_ref[0:1, :], ids_ref[1:2, :]], axis=1)
    block = lax.broadcasted_iota(jnp.int32, (NBLOCK, CAP * NCELL), 0)
    chosen = jnp.where(block == ids, 1.0, 0.0).astype(F32)
    row = jnp.minimum(v, COMP - 1)
    level = lax.broadcasted_iota(jnp.int32, (COMP, BLOCK), 0)
    for b in range(NBLOCK):
        lanes = pl.ds(b * BLOCK, BLOCK)
        for i, ref in enumerate((params_ref, first_ref, second_ref)):
            only = jnp.where(level == row, ref[:, lanes], 0.0)
            mine[i, pl.ds(b, 1), :] = jnp.sum(only, axis=0, keepdims=True)

    pltpu.make_async_copy(grad_ref, rx, recv_sem).wait()

    for p in range(COMP):
        values = jnp.concatenate([rx[:, j, p, :] for j in range(CAP)], axis=0)
        spread[p] = jnp.dot(chosen, values, precision=HIGHEST, preferred_element_type=F32)

    def part(i):
        w = lax.rem(v + i, NVIEW)
        return w, pltpu.make_async_remote_copy(
            src_ref=spread.at[jnp.minimum(w, COMP - 1)],
            dst_ref=shares.at[v],
            send_sem=part_send.at[i],
            recv_sem=part_recv.at[v],
            device_id=(c, w),
            device_id_type=MESH,
        )

    def arrived(buffer, sem, s):
        return pltpu.make_async_copy(buffer.at[s], buffer.at[s], sem.at[s])

    for i in range(1, NVIEW):
        w, copy = part(i)
        pl.when(w < COMP)(copy.start)

    def send_row(i):
        return pltpu.make_async_remote_copy(
            src_ref=rows.at[row],
            dst_ref=rows.at[row],
            send_sem=row_send.at[i],
            recv_sem=row_recv.at[row],
            device_id=(c, lax.rem(v + i, NVIEW)),
            device_id_type=MESH,
        )

    @pl.when(v < COMP)
    def _():
        for s in range(NVIEW):
            pl.when(v != s)(arrived(shares, part_recv, s).wait)
        shares[v] = spread[row]
        grad = shares[0]
        for s in range(1, NVIEW):
            grad = grad + shares[s]
        one = BETA_ONE * mine[1] + (1.0 - BETA_ONE) * grad
        two = BETA_TWO * mine[2] + (1.0 - BETA_TWO) * grad * grad
        fix_one = 1.0 - BETA_ONE**FIRST_STEP
        fix_two = 1.0 - BETA_TWO**FIRST_STEP
        rows[row] = mine[0] - LEARN_RATE * (one / fix_one) / (jnp.sqrt(two / fix_two) + ADAM_EPS)
        for i in range(1, NVIEW):
            send_row(i).start()

    for p in range(COMP):
        pl.when(v != p)(arrived(rows, row_recv, p).wait)
        for b in range(NBLOCK):
            out_ref[pl.ds(p, 1), pl.ds(b * BLOCK, BLOCK)] = rows[p, pl.ds(b, 1), :]

    rest = pl.ds(0, NCELL - 1)
    pltpu.make_async_copy(grad_ref.at[rest], rx.at[rest], send_sem).wait()
    for i in range(1, NVIEW):
        w, copy = part(i)
        pl.when(w < COMP)(copy.wait_send)

    @pl.when(v < COMP)
    def _():
        for i in range(1, NVIEW):
            send_row(i).wait_send()


def shards(
    params, first_moment, second_moment, camera, slot_block, slot_anchor, tile_items, target
):
    vmem = pl.BlockSpec(memory_space=pltpu.VMEM)
    smem = pl.BlockSpec(memory_space=pltpu.SMEM)
    ids = jnp.transpose(slot_block[0, 0, 0], (1, 0))
    anchors = jnp.transpose(slot_anchor[0, 0, 0], (0, 2, 1)).reshape(2 * CAP, NCELL)
    items = jnp.transpose(tile_items[0, 0], (1, 0))
    goals = jnp.transpose(target[0, 0], (1, 0, 2))
    message = (NCELL, CAP, COMP, BLOCK)
    dma = pltpu.SemaphoreType.DMA
    arrived = pl.pallas_call(
        send_blocks,
        out_shape=jax.ShapeDtypeStruct(message, F32),
        in_specs=[smem, smem, smem, vmem],
        out_specs=vmem,
        scratch_shapes=[
            pltpu.VMEM((1 + NBLOCK, COMP, BLOCK), F32),
            pltpu.VMEM(message, F32),
            dma,
            dma,
        ],
        compiler_params=pltpu.CompilerParams(
            collective_id=0, has_side_effects=True, vmem_limit_bytes=24 << 20
        ),
    )(camera[0], ids, anchors, params)
    item_grads, losses = pl.pallas_call(
        render,
        out_shape=[
            jax.ShapeDtypeStruct(message, F32),
            jax.ShapeDtypeStruct((1, TILES), F32),
        ],
        in_specs=[smem, smem, vmem, vmem, vmem],
        out_specs=[vmem, vmem],
        scratch_shapes=[
            pltpu.VMEM((TILES * DEPTH, BLOCK, PIX), F32),
            pltpu.VMEM((5, DEPTH, TILES, PIX), F32),
            pltpu.VMEM((TILES, DEPTH, 8, PIX), F32),
        ],
        compiler_params=pltpu.CompilerParams(vmem_limit_bytes=24 << 20),
    )(camera[0], items, arrived, goals, blur_matrix())
    share = (NVIEW, NBLOCK, BLOCK)
    new_params = pl.pallas_call(
        return_and_step,
        out_shape=jax.ShapeDtypeStruct((COMP, NBLOCK * BLOCK), F32),
        in_specs=[vmem] * 5,
        out_specs=vmem,
        scratch_shapes=[
            pltpu.VMEM(message, F32),
            pltpu.VMEM((COMP, NBLOCK, BLOCK), F32),
            pltpu.VMEM(share, F32),
            pltpu.VMEM((COMP, NBLOCK, BLOCK), F32),
            pltpu.VMEM((3, NBLOCK, BLOCK), F32),
            dma,
            dma,
            dma((NVIEW,)),
            dma((NVIEW,)),
            dma((NVIEW,)),
            dma((NVIEW,)),
        ],
        compiler_params=pltpu.CompilerParams(
            collective_id=1, has_side_effects=True, vmem_limit_bytes=24 << 20
        ),
    )(item_grads, ids, params, first_moment, second_moment)
    return (new_params, losses.reshape(1, 1, TILES))


def solution(mesh):
    placed = (
        P(None, "cell"),
        P(None, "cell"),
        P(None, "cell"),
        P(None, "view", None),
        P(None, "view", "cell", None, None),
        P(None, "view", "cell", None, None, None),
        P(None, "view", "cell", None),
        P(None, "view", "cell", None, None),
    )
    return jax.shard_map(
        shards,
        mesh=mesh,
        in_specs=placed,
        out_specs=(P(None, "cell"), P(None, "view", "cell")),
        check_vma=False,
    )
```

```python
import jax
import jax.numpy as jnp
import numpy as np
from jax import lax
from jax.experimental import pallas as pl
from jax.experimental.pallas import tpu as pltpu
from jax.sharding import PartitionSpec as P

SIDE = 16
PIX = 256
BLOCK = 128
COMP = 7
TAPS = 11
DEPTH = 4
TILES = 8
NCELL = 64
NVIEW = 8
NBLOCK = 64
CAP = 2
NZ = 16
NY = 4
GROUP = 8

SSIM_WEIGHT = 0.2
STABLE_ONE = 0.0001
STABLE_TWO = 0.0009
LEARN_RATE = 0.1
BETA_ONE = 0.9
BETA_TWO = 0.999
ADAM_EPS = 1e-08
FIRST_STEP = 1
OPACITY_CAP = 0.1
WEIGHT_FLOOR = 0.5

F32 = jnp.float32
BF16 = jnp.bfloat16
MESH = pl.DeviceIdType.MESH
HIGHEST = lax.Precision.HIGHEST


def blur_matrix():
    offsets = np.arange(SIDE)[:, None] - np.arange(SIDE)[None, :]
    kernel = np.exp(-(offsets * offsets) / 4.5) * (np.abs(offsets) <= TAPS // 2)
    kernel = kernel / kernel.sum(axis=1, keepdims=True)
    return jnp.asarray(np.kron(kernel, kernel).T, F32)


def cell_peer(i, z, y):
    i = NCELL - 1 - i
    k = lax.div(i, NY)
    m = lax.div(k + 1, 2)
    dz = jnp.where(lax.rem(k, 2) == 1, m, NZ - m)
    return lax.rem(z + dz, NZ) * NY + lax.rem(y + lax.rem(i, NY), NY)


def split(x):
    parts = []
    for _ in range(3):
        part = x.astype(BF16)
        parts.append(part)
        x = x - part.astype(F32)
    return parts


def stack(parts):
    return jnp.concatenate([part.astype(F32) for part in parts], axis=0).astype(BF16)


def product(left, right, dims=((1,), (0,))):
    return lax.dot_general(left, right, (dims, ((), ())), preferred_element_type=F32)


def blurred(rows, table):
    return jnp.dot(rows, table, precision=HIGHEST, preferred_element_type=F32)


def level_of(shape):
    return lax.broadcasted_iota(jnp.int32, shape, 0)


def lane_of(shape):
    return lax.broadcasted_iota(jnp.int32, shape, 1)


def tinted(tile):
    level = level_of((GROUP, BLOCK))
    shifted = jnp.concatenate([tile[4:7], tile[0:5]], axis=0)
    return jnp.where(level == 3, 1.0, jnp.where(level < 3, shifted, 0.0))


def derive(params_ref, camera_ref, derived):
    q0, q1, q2, q3 = (camera_ref[0, i] for i in range(4))
    width = 1024
    derived[0] = jnp.zeros((COMP, BLOCK), F32)
    for part in range(NBLOCK * BLOCK // width):
        values = params_ref[:, pl.ds(part * width, width)]
        row = level_of(values.shape)
        logistic = 1.0 / (1.0 + jnp.exp(-values))
        inverse = 0.5 * jnp.exp(-2.0 * values)
        pos_x, pos_y = values[0:1], values[1:2]
        base_u = (1.0 + q0) * pos_x + q1 * pos_y
        base_w = q2 * pos_x + (1.0 + q3) * pos_y
        out = jnp.where(row == 3, OPACITY_CAP * logistic, logistic)
        out = jnp.where(row == 2, inverse, out)
        out = jnp.where(row == 1, base_w, out)
        out = jnp.where(row == 0, base_u, out)
        for i in range(width // BLOCK):
            derived[1 + part * (width // BLOCK) + i] = out[:, i * BLOCK : (i + 1) * BLOCK]


def forward(items_ref, rx, alphas, merged):
    lane = lane_of((GROUP, 128))
    level = level_of((GROUP, 128))
    level_wide = level_of((GROUP, PIX))
    grid_x = ((lane & (SIDE - 1)).astype(F32) + 0.5) / SIDE
    grid_y = [((lane >> 4).astype(F32) + (0.5 + half * 8)) / SIDE for half in range(2)]
    halves = [pl.ds(0, 128), pl.ds(128, 128)]

    @pl.loop(0, TILES)
    def _(t):
        for k in range(DEPTH):
            tile = rx[items_ref[k, t]]
            cols = jnp.transpose(jnp.concatenate([tile, jnp.zeros((1, BLOCK), F32)], axis=0))
            slot = t * DEPTH + k
            clear = [jnp.ones((GROUP, 128), F32) for _ in range(2)]
            for g in range(BLOCK // GROUP):
                rows = slice(g * GROUP, (g + 1) * GROUP)
                u, w, inverse, opacity = (
                    jnp.broadcast_to(cols[rows, i : i + 1], (GROUP, 128)) for i in range(4)
                )
                dx = grid_x - u
                dx2 = dx * dx
                for half in range(2):
                    dy = grid_y[half] - w
                    alpha = opacity * jnp.exp(-(dx2 + dy * dy) * inverse)
                    alphas[slot, pl.ds(g * GROUP, GROUP), halves[half]] = alpha
                    clear[half] = clear[half] * (1.0 - alpha)
            alpha = alphas[slot]
            first = alpha.astype(BF16)
            second = (alpha - first.astype(F32)).astype(BF16)
            wh, wm, _ = split(tinted(tile))
            both = product(stack([wh, wm]), first)
            rest = product(stack([wh, wh]), second)
            sums = both[0:8] + both[8:16] + rest[0:8]
            for half in range(2):
                p = clear[half]
                for step in (4, 2, 1):
                    p = p * pltpu.roll(p, step, 0)
                merged[0, k, :, halves[half]] = jnp.where(
                    level == t, p, merged[0, k, :, halves[half]]
                )
            for i, at in enumerate((3, 0, 1, 2)):
                merged[1 + i, k] = jnp.where(
                    level_wide == t, sums[at : at + 1], merged[1 + i, k]
                )


def compare(merged, goals, goal_blur, blur_ref, loss_ref, back):
    fronts = [jnp.ones((TILES, PIX), F32)]
    images = [jnp.zeros((TILES, PIX), F32) for _ in range(3)]
    colours = []
    for k in range(DEPTH):
        transmit, total = merged[0, k], merged[1, k]
        scale = (1.0 - transmit) / jnp.maximum(total, WEIGHT_FLOOR)
        shaded = [scale * merged[2 + ch, k] for ch in range(3)]
        images = [images[ch] + fronts[k] * shaded[ch] for ch in range(3)]
        colours.append(shaded)
        fronts.append(fronts[k] * transmit)

    a, b = jnp.concatenate(images, axis=0), goals
    rows = 3 * TILES
    table = blur_ref[...]
    mine = blurred(jnp.concatenate([a, a * a, a * b], axis=0), table)
    ma, saa, sab = (mine[i * rows : (i + 1) * rows] for i in range(3))
    mb, sbb = goal_blur[0:rows], goal_blur[rows:]
    va = saa - ma * ma
    vb = sbb - mb * mb
    cab = sab - ma * mb
    n1 = 2.0 * ma * mb + STABLE_ONE
    n2 = 2.0 * cab + STABLE_TWO
    d1 = ma * ma + mb * mb + STABLE_ONE
    d2 = va + vb + STABLE_TWO
    under = 1.0 / (d1 * d2)
    ssim = n1 * n2 * under
    apart = a - b
    values = (1.0 - SSIM_WEIGHT) * apart * apart + SSIM_WEIGHT * (1.0 - ssim)
    per_tile = values[0:TILES] + values[TILES : 2 * TILES] + values[2 * TILES :]
    count = 3.0 * PIX
    loss = jnp.sum(per_tile, axis=1, keepdims=True) / count
    square = (TILES, TILES)
    loss_ref[...] = jnp.sum(
        jnp.where(level_of(square) == lane_of(square), loss, 0.0), axis=0, keepdims=True
    )

    g_s = -SSIM_WEIGHT / count
    g_n1 = g_s * n2 * under
    g_n2 = g_s * n1 * under
    g_d1 = -g_s * ssim / d1
    g_d2 = -g_s * ssim / d2
    g_ab = 2.0 * g_n2
    g_ma = 2.0 * mb * g_n1 + 2.0 * ma * g_d1 - mb * g_ab - 2.0 * ma * g_d2
    backed = lax.dot_general(
        jnp.concatenate([g_ma, g_d2, g_ab], axis=0),
        table,
        (((1,), (1,)), ((), ())),
        precision=HIGHEST,
        preferred_element_type=F32,
    )
    g_image = (
        (2.0 * (1.0 - SSIM_WEIGHT) / count) * apart
        + backed[0:rows]
        + 2.0 * a * backed[rows : 2 * rows]
        + b * backed[2 * rows :]
    )
    g_ch = [g_image[ch * TILES : (ch + 1) * TILES] for ch in range(3)]
    g_front = jnp.zeros((TILES, PIX), F32)
    for k in reversed(range(DEPTH)):
        transmit, total = merged[0, k], merged[1, k]
        over = 1.0 / jnp.maximum(total, WEIGHT_FLOOR)
        shade = (1.0 - transmit) * over
        lit = sum(g_ch[ch] * merged[2 + ch, k] for ch in range(3)) * over * fronts[k]
        g_transmit = fronts[k] * g_front - lit
        share = jnp.where(total > WEIGHT_FLOOR, 1.0, jnp.where(total == WEIGHT_FLOOR, 0.5, 0.0))
        ways = [fronts[k] * g_ch[ch] * shade for ch in range(3)]
        for i, way in enumerate([*ways, -share * lit * shade, g_transmit * transmit]):
            for t in range(TILES):
                back[t, k, i : i + 1, :] = way[t : t + 1]
        g_front = sum(g_ch[ch] * colours[k][ch] for ch in range(3)) + transmit * g_front


def backward(camera_ref, items_ref, rx, alphas, back, item_grads):
    q0, q1, q2, q3 = (camera_ref[0, i] for i in range(4))
    place = lane_of((16, PIX))
    kind = level_of((16, PIX))
    at_x = ((place & (SIDE - 1)).astype(F32) - 7.5) / SIDE
    at_y = ((place >> 4).astype(F32) - 7.5) / SIDE
    basis = jnp.where(kind == 3, at_x * at_x + at_y * at_y, 0.0)
    basis = jnp.where(kind == 2, at_y, jnp.where(kind == 1, at_x, basis))
    basis = jnp.where(kind == 0, 1.0, basis).astype(BF16)
    along = ((1,), (1,))

    @pl.loop(0, TILES)
    def _(t):
        for k in range(DEPTH):
            tile = rx[items_ref[k, t]]
            slot = t * DEPTH + k
            rays = back[t, k]
            alpha = alphas[slot]
            ah, am, al = split(tinted(tile))
            rh, rm, rl = split(rays)
            slope = product(
                stack([ah, ah, am, am, ah, al]), stack([rh, rm, rh, rm, rl, rh]), ((0,), (0,))
            )
            q = (slope - rays[4:5] / (1.0 - alpha)) * alpha
            moments = sum(product(basis, part, along) for part in split(q))
            first = alpha.astype(BF16)
            second = (alpha - first.astype(F32)).astype(BF16)
            both = product(stack([rh, rm]), first, along)
            tints = both[0:3] + both[8:11] + product(stack([rh, rh]), second, along)[0:3]
            m0, mx, my, mr = (moments[i : i + 1] for i in range(4))
            cu, cw = tile[0:1] - 0.5, tile[1:2] - 0.5
            twice = 2.0 * tile[2:3]
            du = twice * (mx - cu * m0)
            dw = twice * (my - cw * m0)
            spread = mr - 2.0 * (cu * mx + cw * my) + (cu * cu + cw * cw) * m0
            tone = tile[4:7]
            item_grads[slot] = jnp.concatenate(
                [
                    (1.0 + q0) * du + q2 * dw,
                    q1 * du + (1.0 + q3) * dw,
                    twice * spread,
                    (1.0 - tile[3:4] / OPACITY_CAP) * m0,
                    tone * (1.0 - tone) * tints,
                    jnp.zeros((1, BLOCK), F32),
                ],
                axis=0,
            )


def step(
    camera_ref, ids_ref, anchor_ref, items_ref, ids_rows, items_rows, goal_ref, blur_ref,
    params_hbm, first_hbm, second_hbm, out_ref, loss_ref,
    params_ref, first_ref, second_ref, derived, tx, rx, alphas, merged, back, item_grads,
    grads, grads_rx, summed, shares, rows, mine,
    stage_sem, send_sem, recv_sem, back_send, back_recv, part_send, part_recv, row_send, row_recv,
):
    c = lax.axis_index("cell")
    v = lax.axis_index("view")
    z, y = lax.div(c, NY), lax.rem(c, NY)
    staged = [
        pltpu.make_async_copy(source, target, stage_sem.at[i])
        for i, (source, target) in enumerate(
            ((params_hbm, params_ref), (first_hbm, first_ref), (second_hbm, second_ref))
        )
    ]
    for copy in staged:
        copy.start()

    barrier = pltpu.get_barrier_semaphore()

    @pl.loop(0, NCELL - 1, unroll=9)
    def _(i):
        pl.semaphore_signal(
            barrier, inc=1, device_id=(cell_peer(i, z, y), v), device_id_type=MESH
        )

    for i in range(1, NVIEW):
        pl.semaphore_signal(
            barrier, inc=1, device_id=(c, lax.rem(v + i, NVIEW)), device_id_type=MESH
        )

    staged[0].wait()
    derive(params_ref, camera_ref, derived)
    pl.semaphore_wait(barrier, NCELL - 1 + NVIEW - 1)

    def pair(o):
        return pl.ds(o * CAP, CAP)

    def gather(o):
        row = level_of((COMP, BLOCK))
        for j in range(CAP):
            shift = jnp.where(
                row == 0, anchor_ref[j, o], jnp.where(row == 1, anchor_ref[CAP + j, o], 0.0)
            )
            tx[o * CAP + j] = derived[ids_ref[j, o] + 1] + shift

    @pl.loop(0, NCELL - 1, unroll=3)
    def _(i):
        o = cell_peer(i, z, y)
        gather(o)
        pltpu.make_async_remote_copy(
            src_ref=tx.at[pair(o)],
            dst_ref=rx.at[pair(c)],
            send_sem=send_sem,
            recv_sem=recv_sem,
            device_id=(o, v),
            device_id_type=MESH,
        ).start()

    gather(c)
    pltpu.make_async_copy(tx.at[pair(c)], rx.at[pair(c)], recv_sem).start()

    goals = jnp.concatenate([goal_ref[ch] for ch in range(3)], axis=0)
    goal_blur = blurred(jnp.concatenate([goals, goals * goals], axis=0), blur_ref[...])
    ids = jnp.concatenate([ids_rows[0:1, :], ids_rows[1:2, :]], axis=1)
    chosen = jnp.where(level_of((NBLOCK, CAP * NCELL)) == ids, 1.0, 0.0).astype(F32)
    row = jnp.minimum(v, COMP - 1)
    staged[1].wait()
    staged[2].wait()
    level = level_of((COMP, BLOCK))
    for b in range(NBLOCK):
        for i, ref in enumerate((params_ref, first_ref, second_ref)):
            only = jnp.where(level == row, ref[:, pl.ds(b * BLOCK, BLOCK)], 0.0)
            mine[i, pl.ds(b, 1), :] = jnp.sum(only, axis=0, keepdims=True)
    back[...] = jnp.zeros((TILES, DEPTH, GROUP, PIX), F32)
    merged[...] = jnp.zeros((5, DEPTH, TILES, PIX), F32)
    wide = (TILES, TILES * DEPTH * GROUP)
    place = lax.rem(lane_of((1, wide[1])), GROUP).astype(F32)
    for k in range(DEPTH):
        pick = jnp.where(lax.div(lane_of(wide), GROUP) == level_of(wide) * DEPTH + k, 1.0, 0.0)
        entries = jnp.broadcast_to(items_rows[k : k + 1, :].astype(F32), (TILES, TILES))
        place = place + GROUP * product(entries.astype(BF16), pick.astype(BF16))[0:1]

    pltpu.make_async_copy(tx, rx, recv_sem).wait()

    forward(items_ref, rx, alphas, merged)
    compare(merged, goals, goal_blur, blur_ref, loss_ref, back)
    backward(camera_ref, items_ref, rx, alphas, back, item_grads)

    parts = split(item_grads[...].reshape(TILES * DEPTH * GROUP, BLOCK))
    chunk = 256
    for part in range(NCELL * CAP * GROUP // chunk):
        at = (level_of((chunk, wide[1])) + part * chunk).astype(F32)
        spots = jnp.where(at == place, 1.0, 0.0).astype(BF16)
        found = sum(product(spots, x) for x in parts)
        for i in range(chunk // GROUP):
            slot = part * (chunk // GROUP) + i
            grads[slot // CAP, slot % CAP] = found[i * GROUP : i * GROUP + COMP]

    @pl.loop(0, NCELL - 1, unroll=9)
    def _(i):
        o = cell_peer(i, z, y)
        pltpu.make_async_remote_copy(
            src_ref=grads.at[o],
            dst_ref=grads_rx.at[c],
            send_sem=back_send,
            recv_sem=back_recv,
            device_id=(o, v),
            device_id_type=MESH,
        ).start()

    pltpu.make_async_copy(grads.at[c], grads_rx.at[c], back_recv).start()
    pltpu.make_async_copy(grads, grads_rx, back_recv).wait()

    for p in range(COMP):
        values = jnp.concatenate([grads_rx[:, j, p, :] for j in range(CAP)], axis=0)
        summed[p] = jnp.dot(chosen, values, precision=HIGHEST, preferred_element_type=F32)

    def part(i):
        w = lax.rem(v + i, NVIEW)
        return w, pltpu.make_async_remote_copy(
            src_ref=summed.at[jnp.minimum(w, COMP - 1)],
            dst_ref=shares.at[v],
            send_sem=part_send.at[i],
            recv_sem=part_recv.at[v],
            device_id=(c, w),
            device_id_type=MESH,
        )

    def arrived(buffer, sem, s):
        return pltpu.make_async_copy(buffer.at[s], buffer.at[s], sem.at[s])

    for i in range(1, NVIEW):
        w, copy = part(i)
        pl.when(w < COMP)(copy.start)

    def send_row(i):
        return pltpu.make_async_remote_copy(
            src_ref=rows.at[row],
            dst_ref=rows.at[row],
            send_sem=row_send.at[i],
            recv_sem=row_recv.at[row],
            device_id=(c, lax.rem(v + i, NVIEW)),
            device_id_type=MESH,
        )

    @pl.when(v < COMP)
    def _():
        for s in range(NVIEW):
            pl.when(v != s)(arrived(shares, part_recv, s).wait)
        shares[v] = summed[row]
        grad = shares[0]
        for s in range(1, NVIEW):
            grad = grad + shares[s]
        one = BETA_ONE * mine[1] + (1.0 - BETA_ONE) * grad
        two = BETA_TWO * mine[2] + (1.0 - BETA_TWO) * grad * grad
        fix_one = 1.0 - BETA_ONE**FIRST_STEP
        fix_two = 1.0 - BETA_TWO**FIRST_STEP
        rows[row] = mine[0] - LEARN_RATE * (one / fix_one) / (jnp.sqrt(two / fix_two) + ADAM_EPS)
        for i in range(1, NVIEW):
            send_row(i).start()

    for p in range(COMP):
        pl.when(v != p)(arrived(rows, row_recv, p).wait)
        for b in range(NBLOCK):
            out_ref[pl.ds(p, 1), pl.ds(b * BLOCK, BLOCK)] = rows[p, pl.ds(b, 1), :]

    rest = pl.ds(0, CAP * (NCELL - 1))
    pltpu.make_async_copy(tx.at[rest], rx.at[rest], send_sem).wait()
    rest = pl.ds(0, NCELL - 1)
    pltpu.make_async_copy(grads.at[rest], grads_rx.at[rest], back_send).wait()
    for i in range(1, NVIEW):
        w, copy = part(i)
        pl.when(w < COMP)(copy.wait_send)

    @pl.when(v < COMP)
    def _():
        for i in range(1, NVIEW):
            send_row(i).wait_send()


def shards(
    params, first_moment, second_moment, camera, slot_block, slot_anchor, tile_items, target
):
    vmem = pl.BlockSpec(memory_space=pltpu.VMEM)
    smem = pl.BlockSpec(memory_space=pltpu.SMEM)
    hbm = pl.BlockSpec(memory_space=pltpu.HBM)
    ids = jnp.transpose(slot_block[0, 0, 0], (1, 0))
    anchors = jnp.transpose(slot_anchor[0, 0, 0], (0, 2, 1)).reshape(2 * CAP, NCELL)
    items = jnp.transpose(tile_items[0, 0], (1, 0))
    goals = jnp.transpose(target[0, 0], (1, 0, 2))
    message = pltpu.VMEM((NCELL * CAP, COMP, BLOCK), F32)
    returned = pltpu.VMEM((NCELL, CAP, COMP, BLOCK), F32)
    whole = pltpu.VMEM((COMP, NBLOCK * BLOCK), F32)
    table = pltpu.VMEM((COMP, NBLOCK, BLOCK), F32)
    dma = pltpu.SemaphoreType.DMA
    new_params, losses = pl.pallas_call(
        step,
        out_shape=[
            jax.ShapeDtypeStruct((COMP, NBLOCK * BLOCK), F32),
            jax.ShapeDtypeStruct((1, TILES), F32),
        ],
        in_specs=[smem, smem, smem, smem, vmem, vmem, vmem, vmem, hbm, hbm, hbm],
        out_specs=[vmem, vmem],
        scratch_shapes=[
            whole,
            whole,
            whole,
            pltpu.VMEM((1 + NBLOCK, COMP, BLOCK), F32),
            message,
            message,
            pltpu.VMEM((TILES * DEPTH, BLOCK, PIX), F32),
            pltpu.VMEM((5, DEPTH, TILES, PIX), F32),
            pltpu.VMEM((TILES, DEPTH, GROUP, PIX), F32),
            pltpu.VMEM((TILES * DEPTH, GROUP, BLOCK), F32),
            returned,
            returned,
            table,
            pltpu.VMEM((NVIEW, NBLOCK, BLOCK), F32),
            table,
            pltpu.VMEM((3, NBLOCK, BLOCK), F32),
            dma((3,)),
            dma,
            dma,
            dma,
            dma,
            dma((NVIEW,)),
            dma((NVIEW,)),
            dma((NVIEW,)),
            dma((NVIEW,)),
        ],
        compiler_params=pltpu.CompilerParams(
            collective_id=0, has_side_effects=True, vmem_limit_bytes=32 << 20
        ),
    )(
        camera[0], ids, anchors, items, ids, items, goals, blur_matrix(),
        params, first_moment, second_moment,
    )
    return (new_params, losses.reshape(1, 1, TILES))


def solution(mesh):
    placed = (
        P(None, "cell"),
        P(None, "cell"),
        P(None, "cell"),
        P(None, "view", None),
        P(None, "view", "cell", None, None),
        P(None, "view", "cell", None, None, None),
        P(None, "view", "cell", None),
        P(None, "view", "cell", None, None),
    )
    return jax.shard_map(
        shards,
        mesh=mesh,
        in_specs=placed,
        out_specs=(P(None, "cell"), P(None, "view", "cell")),
        check_vma=False,
    )
```

```python
import jax
import jax.numpy as jnp
import numpy as np
from jax import lax
from jax.experimental import pallas as pl
from jax.experimental.pallas import tpu as pltpu
from jax.sharding import PartitionSpec as P

SIDE = 16
PIX = 256
BLOCK = 128
COMP = 7
TAPS = 11
DEPTH = 4
TILES = 8
NCELL = 64
NVIEW = 8
NBLOCK = 64
CAP = 2
NZ = 16
NY = 4
GROUP = 8

SSIM_WEIGHT = 0.2
STABLE_ONE = 0.0001
STABLE_TWO = 0.0009
LEARN_RATE = 0.1
BETA_ONE = 0.9
BETA_TWO = 0.999
ADAM_EPS = 1e-08
FIRST_STEP = 1
OPACITY_CAP = 0.1
WEIGHT_FLOOR = 0.5

F32 = jnp.float32
BF16 = jnp.bfloat16
MESH = pl.DeviceIdType.MESH
HIGHEST = lax.Precision.HIGHEST


def blur_matrix():
    offsets = np.arange(SIDE)[:, None] - np.arange(SIDE)[None, :]
    kernel = np.exp(-(offsets * offsets) / 4.5) * (np.abs(offsets) <= TAPS // 2)
    kernel = kernel / kernel.sum(axis=1, keepdims=True)
    return jnp.asarray(np.kron(kernel, kernel).T, F32)


def cell_peer(i, z, y):
    i = NCELL - 1 - i
    k = lax.div(i, NY)
    m = lax.div(k + 1, 2)
    dz = jnp.where(lax.rem(k, 2) == 1, m, NZ - m)
    return lax.rem(z + dz, NZ) * NY + lax.rem(y + lax.rem(i, NY), NY)


def split(x):
    parts = []
    for _ in range(3):
        part = x.astype(BF16)
        parts.append(part)
        x = x - part.astype(F32)
    return parts


def stack(parts):
    return jnp.concatenate([part.astype(F32) for part in parts], axis=0).astype(BF16)


def product(left, right, dims=((1,), (0,))):
    return lax.dot_general(left, right, (dims, ((), ())), preferred_element_type=F32)


def blurred(rows, table):
    return jnp.dot(rows, table, precision=HIGHEST, preferred_element_type=F32)


def level_of(shape):
    return lax.broadcasted_iota(jnp.int32, shape, 0)


def lane_of(shape):
    return lax.broadcasted_iota(jnp.int32, shape, 1)


def tinted(tile):
    level = level_of((GROUP, BLOCK))
    shifted = jnp.concatenate([tile[4:7], tile[0:5]], axis=0)
    return jnp.where(level == 3, 1.0, jnp.where(level < 3, shifted, 0.0))


def derive(params_ref, camera_ref, derived):
    q0, q1, q2, q3 = (camera_ref[0, i] for i in range(4))
    width = 1024
    derived[0] = jnp.zeros((COMP, BLOCK), F32)
    for part in range(NBLOCK * BLOCK // width):
        values = params_ref[:, pl.ds(part * width, width)]
        row = level_of(values.shape)
        logistic = 1.0 / (1.0 + jnp.exp(-values))
        inverse = 0.5 * jnp.exp(-2.0 * values)
        pos_x, pos_y = values[0:1], values[1:2]
        base_u = (1.0 + q0) * pos_x + q1 * pos_y
        base_w = q2 * pos_x + (1.0 + q3) * pos_y
        out = jnp.where(row == 3, OPACITY_CAP * logistic, logistic)
        out = jnp.where(row == 2, inverse, out)
        out = jnp.where(row == 1, base_w, out)
        out = jnp.where(row == 0, base_u, out)
        for i in range(width // BLOCK):
            derived[1 + part * (width // BLOCK) + i] = out[:, i * BLOCK : (i + 1) * BLOCK]


def forward(items_ref, rx, alphas, merged):
    lane = lane_of((GROUP, 128))
    level = level_of((GROUP, 128))
    level_wide = level_of((GROUP, PIX))
    grid_x = ((lane & (SIDE - 1)).astype(F32) + 0.5) / SIDE
    grid_y = [((lane >> 4).astype(F32) + (0.5 + half * 8)) / SIDE for half in range(2)]
    halves = [pl.ds(0, 128), pl.ds(128, 128)]

    @pl.loop(0, TILES)
    def _(t):
        for k in range(DEPTH):
            tile = rx[items_ref[k, t]]
            cols = jnp.transpose(jnp.concatenate([tile, jnp.zeros((1, BLOCK), F32)], axis=0))
            slot = t * DEPTH + k
            clear = [jnp.ones((GROUP, 128), F32) for _ in range(2)]
            for g in range(BLOCK // GROUP):
                rows = slice(g * GROUP, (g + 1) * GROUP)
                u, w, inverse, opacity = (
                    jnp.broadcast_to(cols[rows, i : i + 1], (GROUP, 128)) for i in range(4)
                )
                dx = grid_x - u
                dx2 = dx * dx
                for half in range(2):
                    dy = grid_y[half] - w
                    alpha = opacity * jnp.exp(-(dx2 + dy * dy) * inverse)
                    alphas[slot, pl.ds(g * GROUP, GROUP), halves[half]] = alpha
                    clear[half] = clear[half] * (1.0 - alpha)
            alpha = alphas[slot]
            first = alpha.astype(BF16)
            second = (alpha - first.astype(F32)).astype(BF16)
            wh, wm, _ = split(tinted(tile))
            both = product(stack([wh, wm]), first)
            rest = product(stack([wh, wh]), second)
            sums = both[0:8] + both[8:16] + rest[0:8]
            for half in range(2):
                p = clear[half]
                for step in (4, 2, 1):
                    p = p * pltpu.roll(p, step, 0)
                merged[0, k, :, halves[half]] = jnp.where(
                    level == t, p, merged[0, k, :, halves[half]]
                )
            for i, at in enumerate((3, 0, 1, 2)):
                merged[1 + i, k] = jnp.where(
                    level_wide == t, sums[at : at + 1], merged[1 + i, k]
                )


def compare(merged, goals, goal_blur, blur_ref, loss_ref, back):
    fronts = [jnp.ones((TILES, PIX), F32)]
    images = [jnp.zeros((TILES, PIX), F32) for _ in range(3)]
    colours = []
    for k in range(DEPTH):
        transmit, total = merged[0, k], merged[1, k]
        scale = (1.0 - transmit) / jnp.maximum(total, WEIGHT_FLOOR)
        shaded = [scale * merged[2 + ch, k] for ch in range(3)]
        images = [images[ch] + fronts[k] * shaded[ch] for ch in range(3)]
        colours.append(shaded)
        fronts.append(fronts[k] * transmit)

    a, b = jnp.concatenate(images, axis=0), goals
    rows = 3 * TILES
    table = blur_ref[...]
    mine = blurred(jnp.concatenate([a, a * a, a * b], axis=0), table)
    ma, saa, sab = (mine[i * rows : (i + 1) * rows] for i in range(3))
    mb, sbb = goal_blur[0:rows], goal_blur[rows:]
    va = saa - ma * ma
    vb = sbb - mb * mb
    cab = sab - ma * mb
    n1 = 2.0 * ma * mb + STABLE_ONE
    n2 = 2.0 * cab + STABLE_TWO
    d1 = ma * ma + mb * mb + STABLE_ONE
    d2 = va + vb + STABLE_TWO
    under = 1.0 / (d1 * d2)
    ssim = n1 * n2 * under
    apart = a - b
    values = (1.0 - SSIM_WEIGHT) * apart * apart + SSIM_WEIGHT * (1.0 - ssim)
    per_tile = values[0:TILES] + values[TILES : 2 * TILES] + values[2 * TILES :]
    count = 3.0 * PIX
    loss = jnp.sum(per_tile, axis=1, keepdims=True) / count
    square = (TILES, TILES)
    loss_ref[...] = jnp.sum(
        jnp.where(level_of(square) == lane_of(square), loss, 0.0), axis=0, keepdims=True
    )

    g_s = -SSIM_WEIGHT / count
    g_n1 = g_s * n2 * under
    g_n2 = g_s * n1 * under
    g_d1 = -g_s * ssim / d1
    g_d2 = -g_s * ssim / d2
    g_ab = 2.0 * g_n2
    g_ma = 2.0 * mb * g_n1 + 2.0 * ma * g_d1 - mb * g_ab - 2.0 * ma * g_d2
    backed = lax.dot_general(
        jnp.concatenate([g_ma, g_d2, g_ab], axis=0),
        table,
        (((1,), (1,)), ((), ())),
        precision=HIGHEST,
        preferred_element_type=F32,
    )
    g_image = (
        (2.0 * (1.0 - SSIM_WEIGHT) / count) * apart
        + backed[0:rows]
        + 2.0 * a * backed[rows : 2 * rows]
        + b * backed[2 * rows :]
    )
    g_ch = [g_image[ch * TILES : (ch + 1) * TILES] for ch in range(3)]
    g_front = jnp.zeros((TILES, PIX), F32)
    for k in reversed(range(DEPTH)):
        transmit, total = merged[0, k], merged[1, k]
        over = 1.0 / jnp.maximum(total, WEIGHT_FLOOR)
        shade = (1.0 - transmit) * over
        lit = sum(g_ch[ch] * merged[2 + ch, k] for ch in range(3)) * over * fronts[k]
        g_transmit = fronts[k] * g_front - lit
        share = jnp.where(total > WEIGHT_FLOOR, 1.0, jnp.where(total == WEIGHT_FLOOR, 0.5, 0.0))
        ways = [fronts[k] * g_ch[ch] * shade for ch in range(3)]
        for i, way in enumerate([*ways, -share * lit * shade, g_transmit * transmit]):
            for t in range(TILES):
                back[t, k, i : i + 1, :] = way[t : t + 1]
        g_front = sum(g_ch[ch] * colours[k][ch] for ch in range(3)) + transmit * g_front


def backward(camera_ref, items_ref, rx, alphas, back, item_grads):
    q0, q1, q2, q3 = (camera_ref[0, i] for i in range(4))
    place = lane_of((16, PIX))
    kind = level_of((16, PIX))
    at_x = ((place & (SIDE - 1)).astype(F32) - 7.5) / SIDE
    at_y = ((place >> 4).astype(F32) - 7.5) / SIDE
    basis = jnp.where(kind == 3, at_x * at_x + at_y * at_y, 0.0)
    basis = jnp.where(kind == 2, at_y, jnp.where(kind == 1, at_x, basis))
    basis = jnp.where(kind == 0, 1.0, basis).astype(BF16)
    along = ((1,), (1,))

    @pl.loop(0, TILES)
    def _(t):
        for k in range(DEPTH):
            tile = rx[items_ref[k, t]]
            slot = t * DEPTH + k
            rays = back[t, k]
            alpha = alphas[slot]
            ah, am, al = split(tinted(tile))
            rh, rm, rl = split(rays)
            slope = product(
                stack([ah, ah, am, am, ah, al]), stack([rh, rm, rh, rm, rl, rh]), ((0,), (0,))
            )
            q = (slope - rays[4:5] / (1.0 - alpha)) * alpha
            moments = sum(product(basis, part, along) for part in split(q))
            first = alpha.astype(BF16)
            second = (alpha - first.astype(F32)).astype(BF16)
            both = product(stack([rh, rm]), first, along)
            tints = both[0:3] + both[8:11] + product(stack([rh, rh]), second, along)[0:3]
            m0, mx, my, mr = (moments[i : i + 1] for i in range(4))
            cu, cw = tile[0:1] - 0.5, tile[1:2] - 0.5
            twice = 2.0 * tile[2:3]
            du = twice * (mx - cu * m0)
            dw = twice * (my - cw * m0)
            spread = mr - 2.0 * (cu * mx + cw * my) + (cu * cu + cw * cw) * m0
            tone = tile[4:7]
            item_grads[slot] = jnp.concatenate(
                [
                    (1.0 + q0) * du + q2 * dw,
                    q1 * du + (1.0 + q3) * dw,
                    twice * spread,
                    (1.0 - tile[3:4] / OPACITY_CAP) * m0,
                    tone * (1.0 - tone) * tints,
                    jnp.zeros((1, BLOCK), F32),
                ],
                axis=0,
            )


def step(
    camera_hbm, anchor_hbm, ids_hbm, items_hbm, goal_hbm, blur_hbm,
    params_hbm, first_hbm, second_hbm, out_ref, loss_ref,
    camera_ref, ids_ref, anchor_ref, items_ref, params_ref, first_ref, second_ref, ids_rows, items_rows, goal_ref, blur_ref, derived, tx, rx, alphas, merged, back, item_grads,
    grads, grads_rx, summed, shares, rows, mine,
    stage_sem, send_sem, recv_sem, back_send, back_recv, part_send, part_recv, row_send, row_recv,
):
    c = lax.axis_index("cell")
    v = lax.axis_index("view")
    z, y = lax.div(c, NY), lax.rem(c, NY)
    staged = [
        pltpu.make_async_copy(source, target, stage_sem.at[i])
        for i, (source, target) in enumerate(
            (
                (params_hbm, params_ref),
                (first_hbm, first_ref),
                (second_hbm, second_ref),
                (ids_hbm, ids_rows),
                (items_hbm, items_rows),
                (goal_hbm, goal_ref),
                (blur_hbm, blur_ref),
                (camera_hbm, camera_ref),
                (ids_hbm, ids_ref),
                (anchor_hbm, anchor_ref),
                (items_hbm, items_ref),
            )
        )
    ]
    for copy in staged:
        copy.start()

    barrier = pltpu.get_barrier_semaphore()

    @pl.loop(0, NCELL - 1, unroll=9)
    def _(i):
        pl.semaphore_signal(
            barrier, inc=1, device_id=(cell_peer(i, z, y), v), device_id_type=MESH
        )

    for i in range(1, NVIEW):
        pl.semaphore_signal(
            barrier, inc=1, device_id=(c, lax.rem(v + i, NVIEW)), device_id_type=MESH
        )

    for i in (0, 7, 8, 9, 10):
        staged[i].wait()
    derive(params_ref, camera_ref, derived)
    pl.semaphore_wait(barrier, NCELL - 1 + NVIEW - 1)

    def pair(o):
        return pl.ds(o * CAP, CAP)

    def gather(o):
        row = level_of((COMP, BLOCK))
        for j in range(CAP):
            shift = jnp.where(
                row == 0, anchor_ref[j, o], jnp.where(row == 1, anchor_ref[CAP + j, o], 0.0)
            )
            tx[o * CAP + j] = derived[ids_ref[j, o] + 1] + shift

    @pl.loop(0, NCELL - 1, unroll=3)
    def _(i):
        o = cell_peer(i, z, y)
        gather(o)
        pltpu.make_async_remote_copy(
            src_ref=tx.at[pair(o)],
            dst_ref=rx.at[pair(c)],
            send_sem=send_sem,
            recv_sem=recv_sem,
            device_id=(o, v),
            device_id_type=MESH,
        ).start()

    gather(c)
    pltpu.make_async_copy(tx.at[pair(c)], rx.at[pair(c)], recv_sem).start()

    for copy in staged[1:7]:
        copy.wait()
    goals = jnp.concatenate([goal_ref[ch] for ch in range(3)], axis=0)
    goal_blur = blurred(jnp.concatenate([goals, goals * goals], axis=0), blur_ref[...])
    ids = jnp.concatenate([ids_rows[0:1, :], ids_rows[1:2, :]], axis=1)
    chosen = jnp.where(level_of((NBLOCK, CAP * NCELL)) == ids, 1.0, 0.0).astype(F32)
    row = jnp.minimum(v, COMP - 1)
    level = level_of((COMP, BLOCK))
    for b in range(NBLOCK):
        for i, ref in enumerate((params_ref, first_ref, second_ref)):
            only = jnp.where(level == row, ref[:, pl.ds(b * BLOCK, BLOCK)], 0.0)
            mine[i, pl.ds(b, 1), :] = jnp.sum(only, axis=0, keepdims=True)
    back[...] = jnp.zeros((TILES, DEPTH, GROUP, PIX), F32)
    merged[...] = jnp.zeros((5, DEPTH, TILES, PIX), F32)
    wide = (TILES, TILES * DEPTH * GROUP)
    place = lax.rem(lane_of((1, wide[1])), GROUP).astype(F32)
    for k in range(DEPTH):
        pick = jnp.where(lax.div(lane_of(wide), GROUP) == level_of(wide) * DEPTH + k, 1.0, 0.0)
        entries = jnp.broadcast_to(items_rows[k : k + 1, :].astype(F32), (TILES, TILES))
        place = place + GROUP * product(entries.astype(BF16), pick.astype(BF16))[0:1]

    pltpu.make_async_copy(tx, rx, recv_sem).wait()

    forward(items_ref, rx, alphas, merged)
    compare(merged, goals, goal_blur, blur_ref, loss_ref, back)
    backward(camera_ref, items_ref, rx, alphas, back, item_grads)

    parts = split(item_grads[...].reshape(TILES * DEPTH * GROUP, BLOCK))
    chunk = 256
    for part in range(NCELL * CAP * GROUP // chunk):
        at = (level_of((chunk, wide[1])) + part * chunk).astype(F32)
        spots = jnp.where(at == place, 1.0, 0.0).astype(BF16)
        found = sum(product(spots, x) for x in parts)
        for i in range(chunk // GROUP):
            slot = part * (chunk // GROUP) + i
            grads[slot // CAP, slot % CAP] = found[i * GROUP : i * GROUP + COMP]

    @pl.loop(0, NCELL - 1, unroll=9)
    def _(i):
        o = cell_peer(i, z, y)
        pltpu.make_async_remote_copy(
            src_ref=grads.at[o],
            dst_ref=grads_rx.at[c],
            send_sem=back_send,
            recv_sem=back_recv,
            device_id=(o, v),
            device_id_type=MESH,
        ).start()

    pltpu.make_async_copy(grads.at[c], grads_rx.at[c], back_recv).start()
    pltpu.make_async_copy(grads, grads_rx, back_recv).wait()

    for p in range(COMP):
        values = jnp.concatenate([grads_rx[:, j, p, :] for j in range(CAP)], axis=0)
        summed[p] = jnp.dot(chosen, values, precision=HIGHEST, preferred_element_type=F32)

    def part(i):
        w = lax.rem(v + i, NVIEW)
        return w, pltpu.make_async_remote_copy(
            src_ref=summed.at[jnp.minimum(w, COMP - 1)],
            dst_ref=shares.at[v],
            send_sem=part_send.at[i],
            recv_sem=part_recv.at[v],
            device_id=(c, w),
            device_id_type=MESH,
        )

    def arrived(buffer, sem, s):
        return pltpu.make_async_copy(buffer.at[s], buffer.at[s], sem.at[s])

    for i in range(1, NVIEW):
        w, copy = part(i)
        pl.when(w < COMP)(copy.start)

    def send_row(i):
        return pltpu.make_async_remote_copy(
            src_ref=rows.at[row],
            dst_ref=rows.at[row],
            send_sem=row_send.at[i],
            recv_sem=row_recv.at[row],
            device_id=(c, lax.rem(v + i, NVIEW)),
            device_id_type=MESH,
        )

    @pl.when(v < COMP)
    def _():
        for s in range(NVIEW):
            pl.when(v != s)(arrived(shares, part_recv, s).wait)
        shares[v] = summed[row]
        grad = shares[0]
        for s in range(1, NVIEW):
            grad = grad + shares[s]
        one = BETA_ONE * mine[1] + (1.0 - BETA_ONE) * grad
        two = BETA_TWO * mine[2] + (1.0 - BETA_TWO) * grad * grad
        fix_one = 1.0 - BETA_ONE**FIRST_STEP
        fix_two = 1.0 - BETA_TWO**FIRST_STEP
        rows[row] = mine[0] - LEARN_RATE * (one / fix_one) / (jnp.sqrt(two / fix_two) + ADAM_EPS)
        for i in range(1, NVIEW):
            send_row(i).start()

    for p in range(COMP):
        pl.when(v != p)(arrived(rows, row_recv, p).wait)
        for b in range(NBLOCK):
            out_ref[pl.ds(p, 1), pl.ds(b * BLOCK, BLOCK)] = rows[p, pl.ds(b, 1), :]

    rest = pl.ds(0, CAP * (NCELL - 1))
    pltpu.make_async_copy(tx.at[rest], rx.at[rest], send_sem).wait()
    rest = pl.ds(0, NCELL - 1)
    pltpu.make_async_copy(grads.at[rest], grads_rx.at[rest], back_send).wait()
    for i in range(1, NVIEW):
        w, copy = part(i)
        pl.when(w < COMP)(copy.wait_send)

    @pl.when(v < COMP)
    def _():
        for i in range(1, NVIEW):
            send_row(i).wait_send()


def shards(
    params, first_moment, second_moment, camera, slot_block, slot_anchor, tile_items, target
):
    vmem = pl.BlockSpec(memory_space=pltpu.VMEM)
    hbm = pl.BlockSpec(memory_space=pltpu.HBM)
    ids = jnp.transpose(slot_block[0, 0, 0], (1, 0))
    anchors = jnp.transpose(slot_anchor[0, 0, 0], (0, 2, 1)).reshape(2 * CAP, NCELL)
    items = jnp.transpose(tile_items[0, 0], (1, 0))
    goals = jnp.transpose(target[0, 0], (1, 0, 2))
    message = pltpu.VMEM((NCELL * CAP, COMP, BLOCK), F32)
    returned = pltpu.VMEM((NCELL, CAP, COMP, BLOCK), F32)
    whole = pltpu.VMEM((COMP, NBLOCK * BLOCK), F32)
    table = pltpu.VMEM((COMP, NBLOCK, BLOCK), F32)
    dma = pltpu.SemaphoreType.DMA
    new_params, losses = pl.pallas_call(
        step,
        out_shape=[
            jax.ShapeDtypeStruct((COMP, NBLOCK * BLOCK), F32),
            jax.ShapeDtypeStruct((1, TILES), F32),
        ],
        in_specs=[hbm] * 9,
        out_specs=[vmem, vmem],
        scratch_shapes=[
            pltpu.SMEM((1, 4), F32),
            pltpu.SMEM((CAP, NCELL), jnp.int32),
            pltpu.SMEM((2 * CAP, NCELL), F32),
            pltpu.SMEM((DEPTH, TILES), jnp.int32),
            whole,
            whole,
            whole,
            pltpu.VMEM((CAP, NCELL), jnp.int32),
            pltpu.VMEM((DEPTH, TILES), jnp.int32),
            pltpu.VMEM((3, TILES, PIX), F32),
            pltpu.VMEM((PIX, PIX), F32),
            pltpu.VMEM((1 + NBLOCK, COMP, BLOCK), F32),
            message,
            message,
            pltpu.VMEM((TILES * DEPTH, BLOCK, PIX), F32),
            pltpu.VMEM((5, DEPTH, TILES, PIX), F32),
            pltpu.VMEM((TILES, DEPTH, GROUP, PIX), F32),
            pltpu.VMEM((TILES * DEPTH, GROUP, BLOCK), F32),
            returned,
            returned,
            table,
            pltpu.VMEM((NVIEW, NBLOCK, BLOCK), F32),
            table,
            pltpu.VMEM((3, NBLOCK, BLOCK), F32),
            dma((11,)),
            dma,
            dma,
            dma,
            dma,
            dma((NVIEW,)),
            dma((NVIEW,)),
            dma((NVIEW,)),
            dma((NVIEW,)),
        ],
        compiler_params=pltpu.CompilerParams(
            collective_id=0, has_side_effects=True, vmem_limit_bytes=56 << 20
        ),
    )(
        camera[0], anchors, ids, items, goals, blur_matrix(),
        params, first_moment, second_moment,
    )
    return (new_params, losses.reshape(1, 1, TILES))


def solution(mesh):
    placed = (
        P(None, "cell"),
        P(None, "cell"),
        P(None, "cell"),
        P(None, "view", None),
        P(None, "view", "cell", None, None),
        P(None, "view", "cell", None, None, None),
        P(None, "view", "cell", None),
        P(None, "view", "cell", None, None),
    )
    return jax.shard_map(
        shards,
        mesh=mesh,
        in_specs=placed,
        out_specs=(P(None, "cell"), P(None, "view", "cell")),
        check_vma=False,
    )
```

```python
import jax
import jax.numpy as jnp
import numpy as np
from jax import lax
from jax.experimental import pallas as pl
from jax.experimental.pallas import tpu as pltpu
from jax.sharding import PartitionSpec as P

SIDE = 16
PIX = 256
BLOCK = 128
COMP = 7
GEO = 4
TINT = 3
EARLY = 42
TAPS = 11
DEPTH = 4
TILES = 8
NCELL = 64
NVIEW = 8
NBLOCK = 64
CAP = 2
NZ = 16
NY = 4
GROUP = 8

SSIM_WEIGHT = 0.2
STABLE_ONE = 0.0001
STABLE_TWO = 0.0009
LEARN_RATE = 0.1
BETA_ONE = 0.9
BETA_TWO = 0.999
ADAM_EPS = 1e-08
FIRST_STEP = 1
OPACITY_CAP = 0.1
WEIGHT_FLOOR = 0.5

F32 = jnp.float32
BF16 = jnp.bfloat16
MESH = pl.DeviceIdType.MESH
HIGHEST = lax.Precision.HIGHEST


def blur_matrix():
    offsets = np.arange(SIDE)[:, None] - np.arange(SIDE)[None, :]
    kernel = np.exp(-(offsets * offsets) / 4.5) * (np.abs(offsets) <= TAPS // 2)
    kernel = kernel / kernel.sum(axis=1, keepdims=True)
    return jnp.asarray(np.kron(kernel, kernel).T, F32)


def cell_peer(i, z, y):
    i = NCELL - 1 - i
    k = lax.div(i, NY)
    m = lax.div(k + 1, 2)
    dz = jnp.where(lax.rem(k, 2) == 1, m, NZ - m)
    return lax.rem(z + dz, NZ) * NY + lax.rem(y + lax.rem(i, NY), NY)


def split(x):
    parts = []
    for _ in range(3):
        part = x.astype(BF16)
        parts.append(part)
        x = x - part.astype(F32)
    return parts


def stack(parts):
    return jnp.concatenate([part.astype(F32) for part in parts], axis=0).astype(BF16)


def product(left, right, dims=((1,), (0,))):
    return lax.dot_general(left, right, (dims, ((), ())), preferred_element_type=F32)


def blurred(rows, table):
    return jnp.dot(rows, table, precision=HIGHEST, preferred_element_type=F32)


def level_of(shape):
    return lax.broadcasted_iota(jnp.int32, shape, 0)


def lane_of(shape):
    return lax.broadcasted_iota(jnp.int32, shape, 1)


def tinted(tile):
    filler = jnp.where(level_of((GROUP - TINT, BLOCK)) == 0, 1.0, 0.0)
    return jnp.concatenate([tile, filler], axis=0)


def item_rows(ref, e, count):
    both = ref[lax.div(e, CAP)]
    second = jnp.full((count, BLOCK), lax.rem(e, CAP), jnp.int32)
    return jnp.where(second == 0, both[:count], both[count:])


def derive(params_ref, camera_ref, shapes, tints):
    q0, q1, q2, q3 = (camera_ref[0, i] for i in range(4))
    width = 1024
    shapes[0] = jnp.zeros((GEO, BLOCK), F32)
    tints[0] = jnp.zeros((TINT, BLOCK), F32)
    for part in range(NBLOCK * BLOCK // width):
        values = params_ref[:, pl.ds(part * width, width)]
        row = level_of(values.shape)
        logistic = 1.0 / (1.0 + jnp.exp(-values))
        inverse = 0.5 * jnp.exp(-2.0 * values)
        pos_x, pos_y = values[0:1], values[1:2]
        base_u = (1.0 + q0) * pos_x + q1 * pos_y
        base_w = q2 * pos_x + (1.0 + q3) * pos_y
        out = jnp.where(row == 3, OPACITY_CAP * logistic, logistic)
        out = jnp.where(row == 2, inverse, out)
        out = jnp.where(row == 1, base_w, out)
        out = jnp.where(row == 0, base_u, out)
        for i in range(width // BLOCK):
            block = 1 + part * (width // BLOCK) + i
            shapes[block] = out[:GEO, i * BLOCK : (i + 1) * BLOCK]
            tints[block] = out[GEO:, i * BLOCK : (i + 1) * BLOCK]


def cover(items_ref, shapes_rx, alphas, firsts, seconds, merged):
    lane = lane_of((GROUP, 128))
    level = level_of((GROUP, 128))
    grid_x = ((lane & (SIDE - 1)).astype(F32) + 0.5) / SIDE
    grid_y = [((lane >> 4).astype(F32) + (0.5 + half * 8)) / SIDE for half in range(2)]
    halves = [pl.ds(0, 128), pl.ds(128, 128)]

    @pl.loop(0, TILES)
    def _(t):
        for k in range(DEPTH):
            tile = item_rows(shapes_rx, items_ref[k, t], GEO)
            cols = jnp.transpose(
                jnp.concatenate([tile, jnp.zeros((GROUP - GEO, BLOCK), F32)], axis=0)
            )
            slot = t * DEPTH + k
            clear = [jnp.ones((GROUP, 128), F32) for _ in range(2)]
            for g in range(BLOCK // GROUP):
                rows = slice(g * GROUP, (g + 1) * GROUP)
                u, w, inverse, opacity = (
                    jnp.broadcast_to(cols[rows, i : i + 1], (GROUP, 128)) for i in range(GEO)
                )
                dx = grid_x - u
                dx2 = dx * dx
                for half in range(2):
                    dy = grid_y[half] - w
                    alpha = opacity * jnp.exp(-(dx2 + dy * dy) * inverse)
                    alphas[slot, pl.ds(g * GROUP, GROUP), halves[half]] = alpha
                    clear[half] = clear[half] * (1.0 - alpha)
            alpha = alphas[slot]
            first = alpha.astype(BF16)
            firsts[slot] = first
            seconds[slot] = (alpha - first.astype(F32)).astype(BF16)
            for half in range(2):
                p = clear[half]
                for step in (4, 2, 1):
                    p = p * pltpu.roll(p, step, 0)
                merged[0, k, :, halves[half]] = jnp.where(
                    level == t, p, merged[0, k, :, halves[half]]
                )


def colour(items_ref, tints_rx, firsts, seconds, merged):
    level_wide = level_of((GROUP, PIX))

    @pl.loop(0, TILES)
    def _(t):
        for k in range(DEPTH):
            slot = t * DEPTH + k
            wh, wm, _ = split(tinted(item_rows(tints_rx, items_ref[k, t], TINT)))
            both = product(stack([wh, wm]), firsts[slot])
            rest = product(stack([wh, wh]), seconds[slot])
            sums = both[0:8] + both[8:16] + rest[0:8]
            for i, at in enumerate((3, 0, 1, 2)):
                merged[1 + i, k] = jnp.where(
                    level_wide == t, sums[at : at + 1], merged[1 + i, k]
                )


def compare(merged, goals, goal_blur, blur_ref, loss_ref, back):
    fronts = [jnp.ones((TILES, PIX), F32)]
    images = [jnp.zeros((TILES, PIX), F32) for _ in range(3)]
    colours = []
    for k in range(DEPTH):
        transmit, total = merged[0, k], merged[1, k]
        scale = (1.0 - transmit) / jnp.maximum(total, WEIGHT_FLOOR)
        shaded = [scale * merged[2 + ch, k] for ch in range(3)]
        images = [images[ch] + fronts[k] * shaded[ch] for ch in range(3)]
        colours.append(shaded)
        fronts.append(fronts[k] * transmit)

    a, b = jnp.concatenate(images, axis=0), goals
    rows = 3 * TILES
    table = blur_ref[...]
    mine = blurred(jnp.concatenate([a, a * a, a * b], axis=0), table)
    ma, saa, sab = (mine[i * rows : (i + 1) * rows] for i in range(3))
    mb, sbb = goal_blur[0:rows], goal_blur[rows:]
    va = saa - ma * ma
    vb = sbb - mb * mb
    cab = sab - ma * mb
    n1 = 2.0 * ma * mb + STABLE_ONE
    n2 = 2.0 * cab + STABLE_TWO
    d1 = ma * ma + mb * mb + STABLE_ONE
    d2 = va + vb + STABLE_TWO
    under = 1.0 / (d1 * d2)
    ssim = n1 * n2 * under
    apart = a - b
    values = (1.0 - SSIM_WEIGHT) * apart * apart + SSIM_WEIGHT * (1.0 - ssim)
    per_tile = values[0:TILES] + values[TILES : 2 * TILES] + values[2 * TILES :]
    count = 3.0 * PIX
    loss = jnp.sum(per_tile, axis=1, keepdims=True) / count
    square = (TILES, TILES)
    loss_ref[0] = jnp.sum(
        jnp.where(level_of(square) == lane_of(square), loss, 0.0), axis=0, keepdims=True
    )

    g_s = -SSIM_WEIGHT / count
    g_n1 = g_s * n2 * under
    g_n2 = g_s * n1 * under
    g_d1 = -g_s * ssim / d1
    g_d2 = -g_s * ssim / d2
    g_ab = 2.0 * g_n2
    g_ma = 2.0 * mb * g_n1 + 2.0 * ma * g_d1 - mb * g_ab - 2.0 * ma * g_d2
    backed = lax.dot_general(
        jnp.concatenate([g_ma, g_d2, g_ab], axis=0),
        table,
        (((1,), (1,)), ((), ())),
        precision=HIGHEST,
        preferred_element_type=F32,
    )
    g_image = (
        (2.0 * (1.0 - SSIM_WEIGHT) / count) * apart
        + backed[0:rows]
        + 2.0 * a * backed[rows : 2 * rows]
        + b * backed[2 * rows :]
    )
    g_ch = [g_image[ch * TILES : (ch + 1) * TILES] for ch in range(3)]
    g_front = jnp.zeros((TILES, PIX), F32)
    for k in reversed(range(DEPTH)):
        transmit, total = merged[0, k], merged[1, k]
        over = 1.0 / jnp.maximum(total, WEIGHT_FLOOR)
        shade = (1.0 - transmit) * over
        lit = sum(g_ch[ch] * merged[2 + ch, k] for ch in range(3)) * over * fronts[k]
        g_transmit = fronts[k] * g_front - lit
        share = jnp.where(total > WEIGHT_FLOOR, 1.0, jnp.where(total == WEIGHT_FLOOR, 0.5, 0.0))
        ways = [fronts[k] * g_ch[ch] * shade for ch in range(3)]
        for i, way in enumerate([*ways, -share * lit * shade, g_transmit * transmit]):
            for t in range(TILES):
                back[t, k, i : i + 1, :] = way[t : t + 1]
        g_front = sum(g_ch[ch] * colours[k][ch] for ch in range(3)) + transmit * g_front


def backward_tints(items_ref, tints_rx, firsts, seconds, back, item_tints):
    along = ((1,), (1,))

    @pl.loop(0, TILES)
    def _(t):
        for k in range(DEPTH):
            tone = item_rows(tints_rx, items_ref[k, t], TINT)
            slot = t * DEPTH + k
            rh, rm, _ = split(back[t, k])
            both = product(stack([rh, rm]), firsts[slot], along)
            rest = product(stack([rh, rh]), seconds[slot], along)
            sums = both[0:TINT] + both[8 : 8 + TINT] + rest[0:TINT]
            item_tints[slot] = jnp.concatenate(
                [tone * (1.0 - tone) * sums, jnp.zeros((1, BLOCK), F32)], axis=0
            )


def backward_shapes(camera_ref, items_ref, shapes_rx, tints_rx, alphas, back, item_shapes):
    q0, q1, q2, q3 = (camera_ref[0, i] for i in range(4))
    place = lane_of((16, PIX))
    kind = level_of((16, PIX))
    at_x = ((place & (SIDE - 1)).astype(F32) - 7.5) / SIDE
    at_y = ((place >> 4).astype(F32) - 7.5) / SIDE
    basis = jnp.where(kind == 3, at_x * at_x + at_y * at_y, 0.0)
    basis = jnp.where(kind == 2, at_y, jnp.where(kind == 1, at_x, basis))
    basis = jnp.where(kind == 0, 1.0, basis).astype(BF16)
    along = ((1,), (1,))

    @pl.loop(0, TILES)
    def _(t):
        for k in range(DEPTH):
            e = items_ref[k, t]
            tile = item_rows(shapes_rx, e, GEO)
            slot = t * DEPTH + k
            rays = back[t, k]
            alpha = alphas[slot]
            ah, am, al = split(tinted(item_rows(tints_rx, e, TINT)))
            rh, rm, rl = split(rays)
            slope = product(
                stack([ah, ah, am, am, ah, al]), stack([rh, rm, rh, rm, rl, rh]), ((0,), (0,))
            )
            q = (slope - rays[4:5] / (1.0 - alpha)) * alpha
            moments = sum(product(basis, part, along) for part in split(q))
            m0, mx, my, mr = (moments[i : i + 1] for i in range(4))
            cu, cw = tile[0:1] - 0.5, tile[1:2] - 0.5
            twice = 2.0 * tile[2:3]
            du = twice * (mx - cu * m0)
            dw = twice * (my - cw * m0)
            spread = mr - 2.0 * (cu * mx + cw * my) + (cu * cu + cw * cw) * m0
            item_shapes[slot] = jnp.concatenate(
                [
                    (1.0 + q0) * du + q2 * dw,
                    q1 * du + (1.0 + q3) * dw,
                    twice * spread,
                    (1.0 - tile[3:4] / OPACITY_CAP) * m0,
                ],
                axis=0,
            )


def to_slots(items, place, out, count):
    parts = split(jnp.concatenate([items[i] for i in range(TILES * DEPTH)], axis=0))
    chunk = 256
    for part in range(NCELL * CAP * GEO // chunk):
        at = (level_of((chunk, TILES * DEPTH * GEO)) + part * chunk).astype(F32)
        spots = jnp.where(at == place, 1.0, 0.0).astype(BF16)
        found = sum(product(spots, x) for x in parts)
        for i in range(chunk // (CAP * GEO)):
            first, second = (found[(CAP * i + j) * GEO :][:count] for j in range(CAP))
            out[part * (chunk // (CAP * GEO)) + i] = jnp.concatenate([first, second], axis=0)


def step(
    camera_hbm, anchor_hbm, ids_hbm, items_hbm, goal_hbm, blur_hbm,
    params_hbm, first_hbm, second_hbm, out_ref, loss_ref,
    camera_ref, ids_ref, anchor_ref, items_ref, params_ref, first_ref, second_ref, ids_rows, items_rows, goal_ref, blur_ref,
    shapes, tints, shapes_tx, tints_tx, shapes_rx, tints_rx, alphas, firsts, seconds, merged, back,
    item_shapes, item_tints, shapes_back, tints_back, shapes_home, tints_home, summed, shares, rows, mine,
    stage_sem, early_send, late_send, shape_recv, tint_send, tint_recv,
    home_tint_send, home_tint_recv, home_send, home_recv, part_send, part_recv, row_send, row_recv,
):
    c = lax.axis_index("cell")
    v = lax.axis_index("view")
    z, y = lax.div(c, NY), lax.rem(c, NY)
    staged = [
        pltpu.make_async_copy(source, target, stage_sem.at[i])
        for i, (source, target) in enumerate(
            (
                (params_hbm, params_ref),
                (first_hbm, first_ref),
                (second_hbm, second_ref),
                (ids_hbm, ids_rows),
                (items_hbm, items_rows),
                (goal_hbm, goal_ref),
                (blur_hbm, blur_ref),
                (camera_hbm, camera_ref),
                (ids_hbm, ids_ref),
                (anchor_hbm, anchor_ref),
                (items_hbm, items_ref),
            )
        )
    ]
    for copy in staged:
        copy.start()

    barrier = pltpu.get_barrier_semaphore()

    @pl.loop(0, NCELL - 1, unroll=9)
    def _(i):
        pl.semaphore_signal(
            barrier, inc=1, device_id=(cell_peer(i, z, y), v), device_id_type=MESH
        )

    for i in range(1, NVIEW):
        pl.semaphore_signal(
            barrier, inc=1, device_id=(c, lax.rem(v + i, NVIEW)), device_id_type=MESH
        )

    for i in (0, 7, 8, 9, 10):
        staged[i].wait()
    derive(params_ref, camera_ref, shapes, tints)
    pl.semaphore_wait(barrier, NCELL - 1 + NVIEW - 1)

    def gather(o):
        row = level_of((GEO, BLOCK))
        blocks = [ids_ref[j, o] + 1 for j in range(CAP)]
        shifts = [
            jnp.where(row == 0, anchor_ref[j, o], jnp.where(row == 1, anchor_ref[CAP + j, o], 0.0))
            for j in range(CAP)
        ]
        shapes_tx[o] = jnp.concatenate([shapes[b] + s for b, s in zip(blocks, shifts)], axis=0)
        tints_tx[o] = jnp.concatenate([tints[b] for b in blocks], axis=0)

    def send(source, target, o, send_sem, recv_sem):
        pltpu.make_async_remote_copy(
            src_ref=source,
            dst_ref=target,
            send_sem=send_sem,
            recv_sem=recv_sem,
            device_id=(o, v),
            device_id_type=MESH,
        ).start()

    for low, high, sem in ((0, EARLY, early_send), (EARLY, NCELL - 1, late_send)):

        @pl.loop(low, high, unroll=3)
        def _(i):
            o = cell_peer(i, z, y)
            gather(o)
            send(shapes_tx.at[o], shapes_rx.at[c], o, sem, shape_recv)

    gather(c)
    pltpu.make_async_copy(shapes_tx.at[c], shapes_rx.at[c], shape_recv).start()

    for copy in staged[1:7]:
        copy.wait()
    goals = jnp.concatenate([goal_ref[ch] for ch in range(3)], axis=0)
    goal_blur = blurred(jnp.concatenate([goals, goals * goals], axis=0), blur_ref[...])
    ids = jnp.concatenate([ids_rows[0:1, :], ids_rows[1:2, :]], axis=1)
    chosen = jnp.where(level_of((NBLOCK, CAP * NCELL)) == ids, 1.0, 0.0).astype(F32)
    row = jnp.minimum(v, COMP - 1)
    level = level_of((COMP, BLOCK))
    for b in range(NBLOCK):
        for i, ref in enumerate((params_ref, first_ref, second_ref)):
            only = jnp.where(level == row, ref[:, pl.ds(b * BLOCK, BLOCK)], 0.0)
            mine[i, pl.ds(b, 1), :] = jnp.sum(only, axis=0, keepdims=True)
    back[...] = jnp.zeros((TILES, DEPTH, GROUP, PIX), F32)
    merged[...] = jnp.zeros((5, DEPTH, TILES, PIX), F32)
    wide = (TILES, TILES * DEPTH * GEO)
    place = lax.rem(lane_of((1, wide[1])), GEO).astype(F32)
    for k in range(DEPTH):
        pick = jnp.where(lax.div(lane_of(wide), GEO) == level_of(wide) * DEPTH + k, 1.0, 0.0)
        entries = jnp.broadcast_to(items_rows[k : k + 1, :].astype(F32), (TILES, TILES))
        place = place + GEO * product(entries.astype(BF16), pick.astype(BF16))[0:1]

    def done(source, target, first, count, sem):
        span = pl.ds(first, count)
        pltpu.make_async_copy(source.at[span], target.at[span], sem).wait()

    done(shapes_tx, shapes_rx, 0, EARLY, early_send)

    @pl.loop(0, NCELL - 1, unroll=9)
    def _(i):
        o = cell_peer(i, z, y)
        send(tints_tx.at[o], tints_rx.at[c], o, tint_send, tint_recv)

    pltpu.make_async_copy(tints_tx.at[c], tints_rx.at[c], tint_recv).start()

    pltpu.make_async_copy(shapes_tx, shapes_rx, shape_recv).wait()
    cover(items_ref, shapes_rx, alphas, firsts, seconds, merged)
    pltpu.make_async_copy(tints_tx, tints_rx, tint_recv).wait()
    colour(items_ref, tints_rx, firsts, seconds, merged)
    compare(merged, goals, goal_blur, blur_ref, loss_ref, back)
    backward_tints(items_ref, tints_rx, firsts, seconds, back, item_tints)
    to_slots(item_tints, place, tints_back, TINT)

    @pl.loop(0, NCELL - 1, unroll=9)
    def _(i):
        o = cell_peer(i, z, y)
        send(tints_back.at[o], tints_home.at[c], o, home_tint_send, home_tint_recv)

    pltpu.make_async_copy(tints_back.at[c], tints_home.at[c], home_tint_recv).start()
    backward_shapes(camera_ref, items_ref, shapes_rx, tints_rx, alphas, back, item_shapes)
    to_slots(item_shapes, place, shapes_back, GEO)

    @pl.loop(0, NCELL - 1, unroll=9)
    def _(i):
        o = cell_peer(i, z, y)
        send(shapes_back.at[o], shapes_home.at[c], o, home_send, home_recv)

    pltpu.make_async_copy(shapes_back.at[c], shapes_home.at[c], home_recv).start()

    def part(i):
        w = lax.rem(v + i, NVIEW)
        return w, pltpu.make_async_remote_copy(
            src_ref=summed.at[jnp.minimum(w, COMP - 1)],
            dst_ref=shares.at[v],
            send_sem=part_send.at[i],
            recv_sem=part_recv.at[v],
            device_id=(c, w),
            device_id_type=MESH,
        )

    def arrived(buffer, sem, s):
        return pltpu.make_async_copy(buffer.at[s], buffer.at[s], sem.at[s])

    for source, target, sem, low, high in (
        (tints_back, tints_home, home_tint_recv, GEO, COMP),
        (shapes_back, shapes_home, home_recv, 0, GEO),
    ):
        pltpu.make_async_copy(source, target, sem).wait()
        for p in range(low, high):
            values = jnp.concatenate(
                [target[:, j * (high - low) + p - low, :] for j in range(CAP)], axis=0
            )
            summed[p] = jnp.dot(chosen, values, precision=HIGHEST, preferred_element_type=F32)
        for i in range(1, NVIEW):
            w, copy = part(i)
            pl.when((w >= low) & (w < high))(copy.start)

    def send_row(i):
        return pltpu.make_async_remote_copy(
            src_ref=rows.at[row],
            dst_ref=rows.at[row],
            send_sem=row_send.at[i],
            recv_sem=row_recv.at[row],
            device_id=(c, lax.rem(v + i, NVIEW)),
            device_id_type=MESH,
        )

    @pl.when(v < COMP)
    def _():
        for s in range(NVIEW):
            pl.when(v != s)(arrived(shares, part_recv, s).wait)
        shares[v] = summed[row]
        grad = shares[0]
        for s in range(1, NVIEW):
            grad = grad + shares[s]
        one = BETA_ONE * mine[1] + (1.0 - BETA_ONE) * grad
        two = BETA_TWO * mine[2] + (1.0 - BETA_TWO) * grad * grad
        fix_one = 1.0 - BETA_ONE**FIRST_STEP
        fix_two = 1.0 - BETA_TWO**FIRST_STEP
        rows[row] = mine[0] - LEARN_RATE * (one / fix_one) / (jnp.sqrt(two / fix_two) + ADAM_EPS)
        for i in range(1, NVIEW):
            send_row(i).start()

    for p in range(COMP):
        pl.when(v != p)(arrived(rows, row_recv, p).wait)
        for b in range(NBLOCK):
            out_ref[pl.ds(p, 1), pl.ds(b * BLOCK, BLOCK)] = rows[p, pl.ds(b, 1), :]

    done(shapes_tx, shapes_rx, 0, NCELL - 1 - EARLY, late_send)
    done(tints_tx, tints_rx, 0, NCELL - 1, tint_send)
    done(tints_back, tints_home, 0, NCELL - 1, home_tint_send)
    done(shapes_back, shapes_home, 0, NCELL - 1, home_send)
    for i in range(1, NVIEW):
        w, copy = part(i)
        pl.when(w < COMP)(copy.wait_send)

    @pl.when(v < COMP)
    def _():
        for i in range(1, NVIEW):
            send_row(i).wait_send()


def shards(
    params, first_moment, second_moment, camera, slot_block, slot_anchor, tile_items, target
):
    vmem = pl.BlockSpec(memory_space=pltpu.VMEM)
    hbm = pl.BlockSpec(memory_space=pltpu.HBM)
    ids = jnp.transpose(slot_block[0, 0, 0], (1, 0))
    anchors = jnp.transpose(slot_anchor[0, 0, 0], (0, 2, 1)).reshape(2 * CAP, NCELL)
    items = jnp.transpose(tile_items[0, 0], (1, 0))
    goals = jnp.transpose(target[0, 0], (1, 0, 2))
    whole = pltpu.VMEM((COMP, NBLOCK * BLOCK), F32)
    table = pltpu.VMEM((COMP, NBLOCK, BLOCK), F32)
    dma = pltpu.SemaphoreType.DMA
    new_params, losses = pl.pallas_call(
        step,
        out_shape=[
            jax.ShapeDtypeStruct((COMP, NBLOCK * BLOCK), F32),
            jax.ShapeDtypeStruct((1, 1, TILES), F32),
        ],
        in_specs=[hbm] * 9,
        out_specs=[vmem, vmem],
        scratch_shapes=[
            pltpu.SMEM((1, 4), F32),
            pltpu.SMEM((CAP, NCELL), jnp.int32),
            pltpu.SMEM((2 * CAP, NCELL), F32),
            pltpu.SMEM((DEPTH, TILES), jnp.int32),
            whole,
            whole,
            whole,
            pltpu.VMEM((CAP, NCELL), jnp.int32),
            pltpu.VMEM((DEPTH, TILES), jnp.int32),
            pltpu.VMEM((3, TILES, PIX), F32),
            pltpu.VMEM((PIX, PIX), F32),
            pltpu.VMEM((1 + NBLOCK, GEO, BLOCK), F32),
            pltpu.VMEM((1 + NBLOCK, TINT, BLOCK), F32),
            pltpu.VMEM((NCELL, CAP * GEO, BLOCK), F32),
            pltpu.VMEM((NCELL, CAP * TINT, BLOCK), F32),
            pltpu.VMEM((NCELL, CAP * GEO, BLOCK), F32),
            pltpu.VMEM((NCELL, CAP * TINT, BLOCK), F32),
            pltpu.VMEM((TILES * DEPTH, BLOCK, PIX), F32),
            pltpu.VMEM((TILES * DEPTH, BLOCK, PIX), BF16),
            pltpu.VMEM((TILES * DEPTH, BLOCK, PIX), BF16),
            pltpu.VMEM((5, DEPTH, TILES, PIX), F32),
            pltpu.VMEM((TILES, DEPTH, GROUP, PIX), F32),
            pltpu.VMEM((TILES * DEPTH, GEO, BLOCK), F32),
            pltpu.VMEM((TILES * DEPTH, GEO, BLOCK), F32),
            pltpu.VMEM((NCELL, CAP * GEO, BLOCK), F32),
            pltpu.VMEM((NCELL, CAP * TINT, BLOCK), F32),
            pltpu.VMEM((NCELL, CAP * GEO, BLOCK), F32),
            pltpu.VMEM((NCELL, CAP * TINT, BLOCK), F32),
            table,
            pltpu.VMEM((NVIEW, NBLOCK, BLOCK), F32),
            table,
            pltpu.VMEM((3, NBLOCK, BLOCK), F32),
            dma((11,)),
            *[dma] * 9,
            dma((NVIEW,)),
            dma((NVIEW,)),
            dma((NVIEW,)),
            dma((NVIEW,)),
        ],
        compiler_params=pltpu.CompilerParams(
            collective_id=0, has_side_effects=True, vmem_limit_bytes=56 << 20
        ),
    )(
        camera[0], anchors, ids, items, goals, blur_matrix(),
        params, first_moment, second_moment,
    )
    return (new_params, losses)


def solution(mesh):
    placed = (
        P(None, "cell"),
        P(None, "cell"),
        P(None, "cell"),
        P(None, "view", None),
        P(None, "view", "cell", None, None),
        P(None, "view", "cell", None, None, None),
        P(None, "view", "cell", None),
        P(None, "view", "cell", None, None),
    )
    return jax.shard_map(
        shards,
        mesh=mesh,
        in_specs=placed,
        out_specs=(P(None, "cell"), P(None, "view", "cell")),
        check_vma=False,
    )
```

```python
import jax
import jax.numpy as jnp
import numpy as np
from jax import lax
from jax.experimental import pallas as pl
from jax.experimental.pallas import tpu as pltpu
from jax.sharding import PartitionSpec as P

SIDE = 16
PIX = 256
BLOCK = 128
COMP = 7
GEO = 4
TINT = 3
EARLY = 42
FAR_FIRST = (4, 3, 5, 2, 6, 7, 1)
TAPS = 11
DEPTH = 4
TILES = 8
NCELL = 64
NVIEW = 8
NBLOCK = 64
CAP = 2
NZ = 16
NY = 4
GROUP = 8

SSIM_WEIGHT = 0.2
STABLE_ONE = 0.0001
STABLE_TWO = 0.0009
LEARN_RATE = 0.1
BETA_ONE = 0.9
BETA_TWO = 0.999
ADAM_EPS = 1e-08
FIRST_STEP = 1
OPACITY_CAP = 0.1
WEIGHT_FLOOR = 0.5

F32 = jnp.float32
BF16 = jnp.bfloat16
MESH = pl.DeviceIdType.MESH
HIGHEST = lax.Precision.HIGHEST


def blur_matrix():
    offsets = np.arange(SIDE)[:, None] - np.arange(SIDE)[None, :]
    kernel = np.exp(-(offsets * offsets) / 4.5) * (np.abs(offsets) <= TAPS // 2)
    kernel = kernel / kernel.sum(axis=1, keepdims=True)
    return jnp.asarray(np.kron(kernel, kernel).T, F32)


def cell_peer(i, z, y):
    i = NCELL - 1 - i
    k = lax.div(i, NY)
    m = lax.div(k + 1, 2)
    dz = jnp.where(lax.rem(k, 2) == 1, m, NZ - m)
    return lax.rem(z + dz, NZ) * NY + lax.rem(y + lax.rem(i, NY), NY)


def row_of(v):
    return lax.div(v, 2) + GEO * lax.rem(v, 2)


def split(x):
    parts = []
    for _ in range(3):
        part = x.astype(BF16)
        parts.append(part)
        x = x - part.astype(F32)
    return parts


def stack(parts):
    return jnp.concatenate([part.astype(F32) for part in parts], axis=0).astype(BF16)


def product(left, right, dims=((1,), (0,))):
    return lax.dot_general(left, right, (dims, ((), ())), preferred_element_type=F32)


def blurred(rows, table):
    return jnp.dot(rows, table, precision=HIGHEST, preferred_element_type=F32)


def level_of(shape):
    return lax.broadcasted_iota(jnp.int32, shape, 0)


def lane_of(shape):
    return lax.broadcasted_iota(jnp.int32, shape, 1)


def tinted(tile):
    filler = jnp.where(level_of((GROUP - TINT, BLOCK)) == 0, 1.0, 0.0)
    return jnp.concatenate([tile, filler], axis=0)


def item_rows(ref, e, count):
    both = ref[lax.div(e, CAP)]
    second = jnp.full((count, BLOCK), lax.rem(e, CAP), jnp.int32)
    return jnp.where(second == 0, both[:count], both[count:])


def derive(params_ref, camera_ref, shapes, tints):
    q0, q1, q2, q3 = (camera_ref[0, i] for i in range(4))
    width = 1024
    shapes[0] = jnp.zeros((GEO, BLOCK), F32)
    tints[0] = jnp.zeros((TINT, BLOCK), F32)
    for part in range(NBLOCK * BLOCK // width):
        values = params_ref[:, pl.ds(part * width, width)]
        row = level_of(values.shape)
        logistic = 1.0 / (1.0 + jnp.exp(-values))
        inverse = 0.5 * jnp.exp(-2.0 * values)
        pos_x, pos_y = values[0:1], values[1:2]
        base_u = (1.0 + q0) * pos_x + q1 * pos_y
        base_w = q2 * pos_x + (1.0 + q3) * pos_y
        out = jnp.where(row == 3, OPACITY_CAP * logistic, logistic)
        out = jnp.where(row == 2, inverse, out)
        out = jnp.where(row == 1, base_w, out)
        out = jnp.where(row == 0, base_u, out)
        for i in range(width // BLOCK):
            block = 1 + part * (width // BLOCK) + i
            shapes[block] = out[:GEO, i * BLOCK : (i + 1) * BLOCK]
            tints[block] = out[GEO:, i * BLOCK : (i + 1) * BLOCK]


def cover(items_ref, shapes_rx, alphas, firsts, seconds, merged):
    lane = lane_of((GROUP, 128))
    level = level_of((GROUP, 128))
    grid_x = ((lane & (SIDE - 1)).astype(F32) + 0.5) / SIDE
    grid_y = [((lane >> 4).astype(F32) + (0.5 + half * 8)) / SIDE for half in range(2)]
    halves = [pl.ds(0, 128), pl.ds(128, 128)]

    @pl.loop(0, TILES)
    def _(t):
        for k in range(DEPTH):
            tile = item_rows(shapes_rx, items_ref[k, t], GEO)
            cols = jnp.transpose(
                jnp.concatenate([tile, jnp.zeros((GROUP - GEO, BLOCK), F32)], axis=0)
            )
            slot = t * DEPTH + k
            clear = [jnp.ones((GROUP, 128), F32) for _ in range(2)]
            for g in range(BLOCK // GROUP):
                rows = slice(g * GROUP, (g + 1) * GROUP)
                u, w, inverse, opacity = (
                    jnp.broadcast_to(cols[rows, i : i + 1], (GROUP, 128)) for i in range(GEO)
                )
                dx = grid_x - u
                dx2 = dx * dx
                for half in range(2):
                    dy = grid_y[half] - w
                    alpha = opacity * jnp.exp(-(dx2 + dy * dy) * inverse)
                    alphas[slot, pl.ds(g * GROUP, GROUP), halves[half]] = alpha
                    clear[half] = clear[half] * (1.0 - alpha)
            alpha = alphas[slot]
            first = alpha.astype(BF16)
            firsts[slot] = first
            seconds[slot] = (alpha - first.astype(F32)).astype(BF16)
            for half in range(2):
                p = clear[half]
                for step in (4, 2, 1):
                    p = p * pltpu.roll(p, step, 0)
                merged[0, k, :, halves[half]] = jnp.where(
                    level == t, p, merged[0, k, :, halves[half]]
                )


def colour(items_ref, tints_rx, firsts, seconds, merged):
    level_wide = level_of((GROUP, PIX))

    @pl.loop(0, TILES)
    def _(t):
        for k in range(DEPTH):
            slot = t * DEPTH + k
            wh, wm, _ = split(tinted(item_rows(tints_rx, items_ref[k, t], TINT)))
            both = product(stack([wh, wm]), firsts[slot])
            rest = product(stack([wh, wh]), seconds[slot])
            sums = both[0:8] + both[8:16] + rest[0:8]
            for i, at in enumerate((3, 0, 1, 2)):
                merged[1 + i, k] = jnp.where(
                    level_wide == t, sums[at : at + 1], merged[1 + i, k]
                )


def compare(merged, goals, goal_blur, blur_ref, loss_ref, back):
    fronts = [jnp.ones((TILES, PIX), F32)]
    images = [jnp.zeros((TILES, PIX), F32) for _ in range(3)]
    colours = []
    for k in range(DEPTH):
        transmit, total = merged[0, k], merged[1, k]
        scale = (1.0 - transmit) / jnp.maximum(total, WEIGHT_FLOOR)
        shaded = [scale * merged[2 + ch, k] for ch in range(3)]
        images = [images[ch] + fronts[k] * shaded[ch] for ch in range(3)]
        colours.append(shaded)
        fronts.append(fronts[k] * transmit)

    a, b = jnp.concatenate(images, axis=0), goals
    rows = 3 * TILES
    table = blur_ref[...]
    mine = blurred(jnp.concatenate([a, a * a, a * b], axis=0), table)
    ma, saa, sab = (mine[i * rows : (i + 1) * rows] for i in range(3))
    mb, sbb = goal_blur[0:rows], goal_blur[rows:]
    va = saa - ma * ma
    vb = sbb - mb * mb
    cab = sab - ma * mb
    n1 = 2.0 * ma * mb + STABLE_ONE
    n2 = 2.0 * cab + STABLE_TWO
    d1 = ma * ma + mb * mb + STABLE_ONE
    d2 = va + vb + STABLE_TWO
    under = 1.0 / (d1 * d2)
    ssim = n1 * n2 * under
    apart = a - b
    values = (1.0 - SSIM_WEIGHT) * apart * apart + SSIM_WEIGHT * (1.0 - ssim)
    per_tile = values[0:TILES] + values[TILES : 2 * TILES] + values[2 * TILES :]
    count = 3.0 * PIX
    loss = jnp.sum(per_tile, axis=1, keepdims=True) / count
    square = (TILES, TILES)
    loss_ref[0] = jnp.sum(
        jnp.where(level_of(square) == lane_of(square), loss, 0.0), axis=0, keepdims=True
    )

    g_s = -SSIM_WEIGHT / count
    g_n1 = g_s * n2 * under
    g_n2 = g_s * n1 * under
    g_d1 = -g_s * ssim / d1
    g_d2 = -g_s * ssim / d2
    g_ab = 2.0 * g_n2
    g_ma = 2.0 * mb * g_n1 + 2.0 * ma * g_d1 - mb * g_ab - 2.0 * ma * g_d2
    backed = lax.dot_general(
        jnp.concatenate([g_ma, g_d2, g_ab], axis=0),
        table,
        (((1,), (1,)), ((), ())),
        precision=HIGHEST,
        preferred_element_type=F32,
    )
    g_image = (
        (2.0 * (1.0 - SSIM_WEIGHT) / count) * apart
        + backed[0:rows]
        + 2.0 * a * backed[rows : 2 * rows]
        + b * backed[2 * rows :]
    )
    g_ch = [g_image[ch * TILES : (ch + 1) * TILES] for ch in range(3)]
    g_front = jnp.zeros((TILES, PIX), F32)
    for k in reversed(range(DEPTH)):
        transmit, total = merged[0, k], merged[1, k]
        over = 1.0 / jnp.maximum(total, WEIGHT_FLOOR)
        shade = (1.0 - transmit) * over
        lit = sum(g_ch[ch] * merged[2 + ch, k] for ch in range(3)) * over * fronts[k]
        g_transmit = fronts[k] * g_front - lit
        share = jnp.where(total > WEIGHT_FLOOR, 1.0, jnp.where(total == WEIGHT_FLOOR, 0.5, 0.0))
        ways = [fronts[k] * g_ch[ch] * shade for ch in range(3)]
        for i, way in enumerate([*ways, -share * lit * shade, g_transmit * transmit]):
            for t in range(TILES):
                back[t, k, i : i + 1, :] = way[t : t + 1]
        g_front = sum(g_ch[ch] * colours[k][ch] for ch in range(3)) + transmit * g_front


def backward_tints(items_ref, tints_rx, firsts, seconds, back, item_tints):
    along = ((1,), (1,))

    @pl.loop(0, TILES)
    def _(t):
        for k in range(DEPTH):
            tone = item_rows(tints_rx, items_ref[k, t], TINT)
            slot = t * DEPTH + k
            rh, rm, _ = split(back[t, k])
            both = product(stack([rh, rm]), firsts[slot], along)
            rest = product(stack([rh, rh]), seconds[slot], along)
            sums = both[0:TINT] + both[8 : 8 + TINT] + rest[0:TINT]
            item_tints[slot] = jnp.concatenate(
                [tone * (1.0 - tone) * sums, jnp.zeros((1, BLOCK), F32)], axis=0
            )


def backward_shapes(camera_ref, items_ref, shapes_rx, tints_rx, alphas, back, item_shapes):
    q0, q1, q2, q3 = (camera_ref[0, i] for i in range(4))
    place = lane_of((16, PIX))
    kind = level_of((16, PIX))
    at_x = ((place & (SIDE - 1)).astype(F32) - 7.5) / SIDE
    at_y = ((place >> 4).astype(F32) - 7.5) / SIDE
    basis = jnp.where(kind == 3, at_x * at_x + at_y * at_y, 0.0)
    basis = jnp.where(kind == 2, at_y, jnp.where(kind == 1, at_x, basis))
    basis = jnp.where(kind == 0, 1.0, basis).astype(BF16)
    along = ((1,), (1,))

    @pl.loop(0, TILES)
    def _(t):
        for k in range(DEPTH):
            e = items_ref[k, t]
            tile = item_rows(shapes_rx, e, GEO)
            slot = t * DEPTH + k
            rays = back[t, k]
            alpha = alphas[slot]
            ah, am, al = split(tinted(item_rows(tints_rx, e, TINT)))
            rh, rm, rl = split(rays)
            slope = product(
                stack([ah, ah, am, am, ah, al]), stack([rh, rm, rh, rm, rl, rh]), ((0,), (0,))
            )
            q = (slope - rays[4:5] / (1.0 - alpha)) * alpha
            moments = sum(product(basis, part, along) for part in split(q))
            m0, mx, my, mr = (moments[i : i + 1] for i in range(4))
            cu, cw = tile[0:1] - 0.5, tile[1:2] - 0.5
            twice = 2.0 * tile[2:3]
            du = twice * (mx - cu * m0)
            dw = twice * (my - cw * m0)
            spread = mr - 2.0 * (cu * mx + cw * my) + (cu * cu + cw * cw) * m0
            item_shapes[slot] = jnp.concatenate(
                [
                    (1.0 + q0) * du + q2 * dw,
                    q1 * du + (1.0 + q3) * dw,
                    twice * spread,
                    (1.0 - tile[3:4] / OPACITY_CAP) * m0,
                ],
                axis=0,
            )


def to_slots(items, place, out, count):
    parts = split(jnp.concatenate([items[i] for i in range(TILES * DEPTH)], axis=0))
    chunk = 256
    for part in range(NCELL * CAP * GEO // chunk):
        at = (level_of((chunk, TILES * DEPTH * GEO)) + part * chunk).astype(F32)
        spots = jnp.where(at == place, 1.0, 0.0).astype(BF16)
        found = sum(product(spots, x) for x in parts)
        for i in range(chunk // (CAP * GEO)):
            first, second = (found[(CAP * i + j) * GEO :][:count] for j in range(CAP))
            out[part * (chunk // (CAP * GEO)) + i] = jnp.concatenate([first, second], axis=0)


def step(
    camera_hbm, anchor_hbm, ids_hbm, items_hbm, goal_hbm, blur_hbm,
    params_hbm, first_hbm, second_hbm, out_ref, loss_ref,
    camera_ref, ids_ref, anchor_ref, items_ref, params_ref, first_ref, second_ref, ids_rows, items_rows, goal_ref, blur_ref,
    shapes, tints, shapes_tx, tints_tx, shapes_rx, tints_rx, alphas, firsts, seconds, merged, back,
    item_shapes, item_tints, shapes_back, tints_back, shapes_home, tints_home, summed, shares, rows, mine,
    stage_sem, early_send, late_send, shape_recv, tint_send, tint_recv,
    home_tint_send, home_tint_recv, home_send, home_recv, part_send, part_recv, row_send, row_recv,
):
    c = lax.axis_index("cell")
    v = lax.axis_index("view")
    z, y = lax.div(c, NY), lax.rem(c, NY)
    staged = [
        pltpu.make_async_copy(source, target, stage_sem.at[i])
        for i, (source, target) in enumerate(
            (
                (params_hbm, params_ref),
                (first_hbm, first_ref),
                (second_hbm, second_ref),
                (ids_hbm, ids_rows),
                (items_hbm, items_rows),
                (goal_hbm, goal_ref),
                (blur_hbm, blur_ref),
                (camera_hbm, camera_ref),
                (ids_hbm, ids_ref),
                (anchor_hbm, anchor_ref),
                (items_hbm, items_ref),
            )
        )
    ]
    for copy in staged:
        copy.start()

    barrier = pltpu.get_barrier_semaphore()

    @pl.loop(0, NCELL - 1, unroll=9)
    def _(i):
        pl.semaphore_signal(
            barrier, inc=1, device_id=(cell_peer(i, z, y), v), device_id_type=MESH
        )

    for i in range(1, NVIEW):
        pl.semaphore_signal(
            barrier, inc=1, device_id=(c, lax.rem(v + i, NVIEW)), device_id_type=MESH
        )

    for i in (0, 7, 8, 9, 10):
        staged[i].wait()
    derive(params_ref, camera_ref, shapes, tints)
    pl.semaphore_wait(barrier, NCELL - 1 + NVIEW - 1)

    def gather_shapes(o):
        row = level_of((GEO, BLOCK))
        shifts = [
            jnp.where(row == 0, anchor_ref[j, o], jnp.where(row == 1, anchor_ref[CAP + j, o], 0.0))
            for j in range(CAP)
        ]
        shapes_tx[o] = jnp.concatenate(
            [shapes[ids_ref[j, o] + 1] + shifts[j] for j in range(CAP)], axis=0
        )

    def gather_tints(o):
        tints_tx[o] = jnp.concatenate([tints[ids_ref[j, o] + 1] for j in range(CAP)], axis=0)

    def send(source, target, o, send_sem, recv_sem):
        pltpu.make_async_remote_copy(
            src_ref=source,
            dst_ref=target,
            send_sem=send_sem,
            recv_sem=recv_sem,
            device_id=(o, v),
            device_id_type=MESH,
        ).start()

    for low, high, sem in ((0, EARLY, early_send), (EARLY, NCELL - 1, late_send)):

        @pl.loop(low, high, unroll=3)
        def _(i):
            o = cell_peer(i, z, y)
            gather_shapes(o)
            send(shapes_tx.at[o], shapes_rx.at[c], o, sem, shape_recv)

    gather_shapes(c)
    pltpu.make_async_copy(shapes_tx.at[c], shapes_rx.at[c], shape_recv).start()

    for copy in staged[1:7]:
        copy.wait()
    goals = jnp.concatenate([goal_ref[ch] for ch in range(3)], axis=0)
    goal_blur = blurred(jnp.concatenate([goals, goals * goals], axis=0), blur_ref[...])
    ids = jnp.concatenate([ids_rows[0:1, :], ids_rows[1:2, :]], axis=1)
    chosen = jnp.where(level_of((NBLOCK, CAP * NCELL)) == ids, 1.0, 0.0).astype(F32)
    own = row_of(v)
    row = jnp.minimum(own, COMP - 1)
    level = level_of((COMP, BLOCK))
    for b in range(NBLOCK):
        for i, ref in enumerate((params_ref, first_ref, second_ref)):
            only = jnp.where(level == row, ref[:, pl.ds(b * BLOCK, BLOCK)], 0.0)
            mine[i, pl.ds(b, 1), :] = jnp.sum(only, axis=0, keepdims=True)
    back[...] = jnp.zeros((TILES, DEPTH, GROUP, PIX), F32)
    merged[...] = jnp.zeros((5, DEPTH, TILES, PIX), F32)
    wide = (TILES, TILES * DEPTH * GEO)
    place = lax.rem(lane_of((1, wide[1])), GEO).astype(F32)
    for k in range(DEPTH):
        pick = jnp.where(lax.div(lane_of(wide), GEO) == level_of(wide) * DEPTH + k, 1.0, 0.0)
        entries = jnp.broadcast_to(items_rows[k : k + 1, :].astype(F32), (TILES, TILES))
        place = place + GEO * product(entries.astype(BF16), pick.astype(BF16))[0:1]

    def done(source, target, first, count, sem):
        span = pl.ds(first, count)
        pltpu.make_async_copy(source.at[span], target.at[span], sem).wait()

    done(shapes_tx, shapes_rx, 0, EARLY, early_send)

    @pl.loop(0, NCELL - 1, unroll=3)
    def _(i):
        o = cell_peer(i, z, y)
        gather_tints(o)
        send(tints_tx.at[o], tints_rx.at[c], o, tint_send, tint_recv)

    gather_tints(c)
    pltpu.make_async_copy(tints_tx.at[c], tints_rx.at[c], tint_recv).start()

    pltpu.make_async_copy(shapes_tx, shapes_rx, shape_recv).wait()
    cover(items_ref, shapes_rx, alphas, firsts, seconds, merged)
    pltpu.make_async_copy(tints_tx, tints_rx, tint_recv).wait()
    colour(items_ref, tints_rx, firsts, seconds, merged)
    compare(merged, goals, goal_blur, blur_ref, loss_ref, back)
    backward_tints(items_ref, tints_rx, firsts, seconds, back, item_tints)
    to_slots(item_tints, place, tints_back, TINT)

    @pl.loop(0, NCELL - 1, unroll=9)
    def _(i):
        o = cell_peer(i, z, y)
        send(tints_back.at[o], tints_home.at[c], o, home_tint_send, home_tint_recv)

    pltpu.make_async_copy(tints_back.at[c], tints_home.at[c], home_tint_recv).start()
    backward_shapes(camera_ref, items_ref, shapes_rx, tints_rx, alphas, back, item_shapes)
    to_slots(item_shapes, place, shapes_back, GEO)

    @pl.loop(0, NCELL - 1, unroll=9)
    def _(i):
        o = cell_peer(i, z, y)
        send(shapes_back.at[o], shapes_home.at[c], o, home_send, home_recv)

    pltpu.make_async_copy(shapes_back.at[c], shapes_home.at[c], home_recv).start()

    def part(i):
        w = lax.rem(v + i, NVIEW)
        return w, pltpu.make_async_remote_copy(
            src_ref=summed.at[jnp.minimum(row_of(w), COMP - 1)],
            dst_ref=shares.at[v],
            send_sem=part_send.at[i],
            recv_sem=part_recv.at[v],
            device_id=(c, w),
            device_id_type=MESH,
        )

    def arrived(buffer, sem, s):
        return pltpu.make_async_copy(buffer.at[s], buffer.at[s], sem.at[s])

    for source, target, sem, low, high in (
        (tints_back, tints_home, home_tint_recv, GEO, COMP),
        (shapes_back, shapes_home, home_recv, 0, GEO),
    ):
        pltpu.make_async_copy(source, target, sem).wait()
        for p in range(low, high):
            values = jnp.concatenate(
                [target[:, j * (high - low) + p - low, :] for j in range(CAP)], axis=0
            )
            summed[p] = jnp.dot(chosen, values, precision=HIGHEST, preferred_element_type=F32)
        for i in FAR_FIRST:
            w, copy = part(i)
            pl.when((row_of(w) >= low) & (row_of(w) < high))(copy.start)

    def send_row(i):
        return pltpu.make_async_remote_copy(
            src_ref=rows.at[row],
            dst_ref=rows.at[row],
            send_sem=row_send.at[i],
            recv_sem=row_recv.at[row],
            device_id=(c, lax.rem(v + i, NVIEW)),
            device_id_type=MESH,
        )

    @pl.when(v < COMP)
    def _():
        for s in range(NVIEW):
            pl.when(v != s)(arrived(shares, part_recv, s).wait)
        shares[v] = summed[row]
        grad = shares[0]
        for s in range(1, NVIEW):
            grad = grad + shares[s]
        one = BETA_ONE * mine[1] + (1.0 - BETA_ONE) * grad
        two = BETA_TWO * mine[2] + (1.0 - BETA_TWO) * grad * grad
        fix_one = 1.0 - BETA_ONE**FIRST_STEP
        fix_two = 1.0 - BETA_TWO**FIRST_STEP
        rows[row] = mine[0] - LEARN_RATE * (one / fix_one) / (jnp.sqrt(two / fix_two) + ADAM_EPS)
        for i in FAR_FIRST:
            send_row(i).start()

    for p in (*range(GEO, COMP), *range(GEO)):
        pl.when(own != p)(arrived(rows, row_recv, p).wait)
        for b in range(NBLOCK):
            out_ref[pl.ds(p, 1), pl.ds(b * BLOCK, BLOCK)] = rows[p, pl.ds(b, 1), :]

    done(shapes_tx, shapes_rx, 0, NCELL - 1 - EARLY, late_send)
    done(tints_tx, tints_rx, 0, NCELL - 1, tint_send)
    done(tints_back, tints_home, 0, NCELL - 1, home_tint_send)
    done(shapes_back, shapes_home, 0, NCELL - 1, home_send)
    for i in range(1, NVIEW):
        w, copy = part(i)
        pl.when(w < COMP)(copy.wait_send)

    @pl.when(v < COMP)
    def _():
        for i in range(1, NVIEW):
            send_row(i).wait_send()


def shards(
    params, first_moment, second_moment, camera, slot_block, slot_anchor, tile_items, target
):
    vmem = pl.BlockSpec(memory_space=pltpu.VMEM)
    hbm = pl.BlockSpec(memory_space=pltpu.HBM)
    ids = jnp.transpose(slot_block[0, 0, 0], (1, 0))
    anchors = jnp.transpose(slot_anchor[0, 0, 0], (0, 2, 1)).reshape(2 * CAP, NCELL)
    items = jnp.transpose(tile_items[0, 0], (1, 0))
    goals = jnp.transpose(target[0, 0], (1, 0, 2))
    whole = pltpu.VMEM((COMP, NBLOCK * BLOCK), F32)
    table = pltpu.VMEM((COMP, NBLOCK, BLOCK), F32)
    dma = pltpu.SemaphoreType.DMA
    new_params, losses = pl.pallas_call(
        step,
        out_shape=[
            jax.ShapeDtypeStruct((COMP, NBLOCK * BLOCK), F32),
            jax.ShapeDtypeStruct((1, 1, TILES), F32),
        ],
        in_specs=[hbm] * 9,
        out_specs=[vmem, vmem],
        scratch_shapes=[
            pltpu.SMEM((1, 4), F32),
            pltpu.SMEM((CAP, NCELL), jnp.int32),
            pltpu.SMEM((2 * CAP, NCELL), F32),
            pltpu.SMEM((DEPTH, TILES), jnp.int32),
            whole,
            whole,
            whole,
            pltpu.VMEM((CAP, NCELL), jnp.int32),
            pltpu.VMEM((DEPTH, TILES), jnp.int32),
            pltpu.VMEM((3, TILES, PIX), F32),
            pltpu.VMEM((PIX, PIX), F32),
            pltpu.VMEM((1 + NBLOCK, GEO, BLOCK), F32),
            pltpu.VMEM((1 + NBLOCK, TINT, BLOCK), F32),
            pltpu.VMEM((NCELL, CAP * GEO, BLOCK), F32),
            pltpu.VMEM((NCELL, CAP * TINT, BLOCK), F32),
            pltpu.VMEM((NCELL, CAP * GEO, BLOCK), F32),
            pltpu.VMEM((NCELL, CAP * TINT, BLOCK), F32),
            pltpu.VMEM((TILES * DEPTH, BLOCK, PIX), F32),
            pltpu.VMEM((TILES * DEPTH, BLOCK, PIX), BF16),
            pltpu.VMEM((TILES * DEPTH, BLOCK, PIX), BF16),
            pltpu.VMEM((5, DEPTH, TILES, PIX), F32),
            pltpu.VMEM((TILES, DEPTH, GROUP, PIX), F32),
            pltpu.VMEM((TILES * DEPTH, GEO, BLOCK), F32),
            pltpu.VMEM((TILES * DEPTH, GEO, BLOCK), F32),
            pltpu.VMEM((NCELL, CAP * GEO, BLOCK), F32),
            pltpu.VMEM((NCELL, CAP * TINT, BLOCK), F32),
            pltpu.VMEM((NCELL, CAP * GEO, BLOCK), F32),
            pltpu.VMEM((NCELL, CAP * TINT, BLOCK), F32),
            table,
            pltpu.VMEM((NVIEW, NBLOCK, BLOCK), F32),
            table,
            pltpu.VMEM((3, NBLOCK, BLOCK), F32),
            dma((11,)),
            *[dma] * 9,
            dma((NVIEW,)),
            dma((NVIEW,)),
            dma((NVIEW,)),
            dma((NVIEW,)),
        ],
        compiler_params=pltpu.CompilerParams(
            collective_id=0, has_side_effects=True, vmem_limit_bytes=56 << 20
        ),
    )(
        camera[0], anchors, ids, items, goals, blur_matrix(),
        params, first_moment, second_moment,
    )
    return (new_params, losses)


def solution(mesh):
    placed = (
        P(None, "cell"),
        P(None, "cell"),
        P(None, "cell"),
        P(None, "view", None),
        P(None, "view", "cell", None, None),
        P(None, "view", "cell", None, None, None),
        P(None, "view", "cell", None),
        P(None, "view", "cell", None, None),
    )
    return jax.shard_map(
        shards,
        mesh=mesh,
        in_specs=placed,
        out_specs=(P(None, "cell"), P(None, "view", "cell")),
        check_vma=False,
    )
```

```python
import jax
import jax.numpy as jnp
import numpy as np
from jax import lax
from jax.experimental import pallas as pl
from jax.experimental.pallas import tpu as pltpu
from jax.sharding import PartitionSpec as P

SIDE = 16
PIX = 256
BLOCK = 128
COMP = 7
GEO = 4
TINT = 3
EARLY = 42
FAR_FIRST = (4, 3, 5, 2, 6, 7, 1)
TAPS = 11
DEPTH = 4
TILES = 8
NCELL = 64
NVIEW = 8
NBLOCK = 64
CAP = 2
NZ = 16
NY = 4
GROUP = 8

SSIM_WEIGHT = 0.2
STABLE_ONE = 0.0001
STABLE_TWO = 0.0009
LEARN_RATE = 0.1
BETA_ONE = 0.9
BETA_TWO = 0.999
ADAM_EPS = 1e-08
FIRST_STEP = 1
OPACITY_CAP = 0.1
WEIGHT_FLOOR = 0.5

F32 = jnp.float32
BF16 = jnp.bfloat16
MESH = pl.DeviceIdType.MESH
HIGHEST = lax.Precision.HIGHEST


def blur_matrix():
    offsets = np.arange(SIDE)[:, None] - np.arange(SIDE)[None, :]
    kernel = np.exp(-(offsets * offsets) / 4.5) * (np.abs(offsets) <= TAPS // 2)
    kernel = kernel / kernel.sum(axis=1, keepdims=True)
    return jnp.asarray(np.kron(kernel, kernel).T, F32)


def cell_peer(i, z, y):
    i = NCELL - 1 - i
    k = lax.div(i, NY)
    m = lax.div(k + 1, 2)
    dz = jnp.where(lax.rem(k, 2) == 1, m, NZ - m)
    return lax.rem(z + dz, NZ) * NY + lax.rem(y + lax.rem(i, NY), NY)


def row_of(v):
    return lax.div(v, 2) + GEO * lax.rem(v, 2)


def split(x):
    parts = []
    for _ in range(3):
        part = x.astype(BF16)
        parts.append(part)
        x = x - part.astype(F32)
    return parts


def stack(parts):
    return jnp.concatenate([part.astype(F32) for part in parts], axis=0).astype(BF16)


def product(left, right, dims=((1,), (0,))):
    return lax.dot_general(left, right, (dims, ((), ())), preferred_element_type=F32)


def blurred(rows, table):
    return jnp.dot(rows, table, precision=HIGHEST, preferred_element_type=F32)


def level_of(shape):
    return lax.broadcasted_iota(jnp.int32, shape, 0)


def lane_of(shape):
    return lax.broadcasted_iota(jnp.int32, shape, 1)


def tinted(tile):
    filler = jnp.where(level_of((GROUP - TINT, BLOCK)) == 0, 1.0, 0.0)
    return jnp.concatenate([tile, filler], axis=0)


def item_rows(ref, e, count):
    both = ref[lax.div(e, CAP)]
    second = jnp.full((count, BLOCK), lax.rem(e, CAP), jnp.int32)
    return jnp.where(second == 0, both[:count], both[count:])


def derive(params_ref, camera_ref, shapes, tints):
    q0, q1, q2, q3 = (camera_ref[0, i] for i in range(4))
    width = 1024
    shapes[0] = jnp.zeros((GEO, BLOCK), F32)
    tints[0] = jnp.zeros((TINT, BLOCK), F32)
    for part in range(NBLOCK * BLOCK // width):
        values = params_ref[:, pl.ds(part * width, width)]
        row = level_of(values.shape)
        logistic = 1.0 / (1.0 + jnp.exp(-values))
        inverse = 0.5 * jnp.exp(-2.0 * values)
        pos_x, pos_y = values[0:1], values[1:2]
        base_u = (1.0 + q0) * pos_x + q1 * pos_y
        base_w = q2 * pos_x + (1.0 + q3) * pos_y
        out = jnp.where(row == 3, OPACITY_CAP * logistic, logistic)
        out = jnp.where(row == 2, inverse, out)
        out = jnp.where(row == 1, base_w, out)
        out = jnp.where(row == 0, base_u, out)
        for i in range(width // BLOCK):
            block = 1 + part * (width // BLOCK) + i
            shapes[block] = out[:GEO, i * BLOCK : (i + 1) * BLOCK]
            tints[block] = out[GEO:, i * BLOCK : (i + 1) * BLOCK]


def cover(items_ref, shapes_rx, alphas, firsts, seconds, merged):
    lane = lane_of((GROUP, 128))
    level = level_of((GROUP, 128))
    grid_x = ((lane & (SIDE - 1)).astype(F32) + 0.5) / SIDE
    grid_y = [((lane >> 4).astype(F32) + (0.5 + half * 8)) / SIDE for half in range(2)]
    halves = [pl.ds(0, 128), pl.ds(128, 128)]

    @pl.loop(0, TILES)
    def _(t):
        for k in range(DEPTH):
            tile = item_rows(shapes_rx, items_ref[k, t], GEO)
            cols = jnp.transpose(
                jnp.concatenate([tile, jnp.zeros((GROUP - GEO, BLOCK), F32)], axis=0)
            )
            slot = t * DEPTH + k
            clear = [jnp.ones((GROUP, 128), F32) for _ in range(2)]
            for g in range(BLOCK // GROUP):
                rows = slice(g * GROUP, (g + 1) * GROUP)
                u, w, inverse, opacity = (
                    jnp.broadcast_to(cols[rows, i : i + 1], (GROUP, 128)) for i in range(GEO)
                )
                dx = grid_x - u
                dx2 = dx * dx
                for half in range(2):
                    dy = grid_y[half] - w
                    alpha = opacity * jnp.exp(-(dx2 + dy * dy) * inverse)
                    alphas[slot, pl.ds(g * GROUP, GROUP), halves[half]] = alpha
                    clear[half] = clear[half] * (1.0 - alpha)
            alpha = alphas[slot]
            first = alpha.astype(BF16)
            firsts[slot] = first
            seconds[slot] = (alpha - first.astype(F32)).astype(BF16)
            for half in range(2):
                p = clear[half]
                for step in (4, 2, 1):
                    p = p * pltpu.roll(p, step, 0)
                merged[0, k, :, halves[half]] = jnp.where(
                    level == t, p, merged[0, k, :, halves[half]]
                )


def colour(items_ref, tints_rx, firsts, seconds, merged):
    level_wide = level_of((GROUP, PIX))

    @pl.loop(0, TILES)
    def _(t):
        for k in range(DEPTH):
            slot = t * DEPTH + k
            wh, wm, _ = split(tinted(item_rows(tints_rx, items_ref[k, t], TINT)))
            both = product(stack([wh, wm]), firsts[slot])
            rest = product(stack([wh, wh]), seconds[slot])
            sums = both[0:8] + both[8:16] + rest[0:8]
            for i, at in enumerate((3, 0, 1, 2)):
                merged[1 + i, k] = jnp.where(
                    level_wide == t, sums[at : at + 1], merged[1 + i, k]
                )


def compare(merged, goals, goal_blur, blur_ref, loss_ref, back):
    fronts = [jnp.ones((TILES, PIX), F32)]
    images = [jnp.zeros((TILES, PIX), F32) for _ in range(3)]
    colours = []
    for k in range(DEPTH):
        transmit, total = merged[0, k], merged[1, k]
        scale = (1.0 - transmit) / jnp.maximum(total, WEIGHT_FLOOR)
        shaded = [scale * merged[2 + ch, k] for ch in range(3)]
        images = [images[ch] + fronts[k] * shaded[ch] for ch in range(3)]
        colours.append(shaded)
        fronts.append(fronts[k] * transmit)

    a, b = jnp.concatenate(images, axis=0), goals
    rows = 3 * TILES
    table = blur_ref[...]
    mine = blurred(jnp.concatenate([a, a * a, a * b], axis=0), table)
    ma, saa, sab = (mine[i * rows : (i + 1) * rows] for i in range(3))
    mb, sbb = goal_blur[0:rows], goal_blur[rows:]
    va = saa - ma * ma
    vb = sbb - mb * mb
    cab = sab - ma * mb
    n1 = 2.0 * ma * mb + STABLE_ONE
    n2 = 2.0 * cab + STABLE_TWO
    d1 = ma * ma + mb * mb + STABLE_ONE
    d2 = va + vb + STABLE_TWO
    under = 1.0 / (d1 * d2)
    ssim = n1 * n2 * under
    apart = a - b
    values = (1.0 - SSIM_WEIGHT) * apart * apart + SSIM_WEIGHT * (1.0 - ssim)
    per_tile = values[0:TILES] + values[TILES : 2 * TILES] + values[2 * TILES :]
    count = 3.0 * PIX
    loss = jnp.sum(per_tile, axis=1, keepdims=True) / count
    square = (TILES, TILES)
    loss_ref[0] = jnp.sum(
        jnp.where(level_of(square) == lane_of(square), loss, 0.0), axis=0, keepdims=True
    )

    g_s = -SSIM_WEIGHT / count
    g_n1 = g_s * n2 * under
    g_n2 = g_s * n1 * under
    g_d1 = -g_s * ssim / d1
    g_d2 = -g_s * ssim / d2
    g_ab = 2.0 * g_n2
    g_ma = 2.0 * mb * g_n1 + 2.0 * ma * g_d1 - mb * g_ab - 2.0 * ma * g_d2
    backed = lax.dot_general(
        jnp.concatenate([g_ma, g_d2, g_ab], axis=0),
        table,
        (((1,), (1,)), ((), ())),
        precision=HIGHEST,
        preferred_element_type=F32,
    )
    g_image = (
        (2.0 * (1.0 - SSIM_WEIGHT) / count) * apart
        + backed[0:rows]
        + 2.0 * a * backed[rows : 2 * rows]
        + b * backed[2 * rows :]
    )
    g_ch = [g_image[ch * TILES : (ch + 1) * TILES] for ch in range(3)]
    g_front = jnp.zeros((TILES, PIX), F32)
    for k in reversed(range(DEPTH)):
        transmit, total = merged[0, k], merged[1, k]
        over = 1.0 / jnp.maximum(total, WEIGHT_FLOOR)
        shade = (1.0 - transmit) * over
        lit = sum(g_ch[ch] * merged[2 + ch, k] for ch in range(3)) * over * fronts[k]
        g_transmit = fronts[k] * g_front - lit
        share = jnp.where(total > WEIGHT_FLOOR, 1.0, jnp.where(total == WEIGHT_FLOOR, 0.5, 0.0))
        ways = [fronts[k] * g_ch[ch] * shade for ch in range(3)]
        for i, way in enumerate([*ways, -share * lit * shade, g_transmit * transmit]):
            for t in range(TILES):
                back[t, k, i : i + 1, :] = way[t : t + 1]
        g_front = sum(g_ch[ch] * colours[k][ch] for ch in range(3)) + transmit * g_front


def backward_tints(items_ref, tints_rx, firsts, seconds, back, item_tints):
    along = ((1,), (1,))

    @pl.loop(0, TILES)
    def _(t):
        for k in range(DEPTH):
            tone = item_rows(tints_rx, items_ref[k, t], TINT)
            slot = t * DEPTH + k
            rh, rm, _ = split(back[t, k])
            both = product(stack([rh, rm]), firsts[slot], along)
            rest = product(stack([rh, rh]), seconds[slot], along)
            sums = both[0:TINT] + both[8 : 8 + TINT] + rest[0:TINT]
            item_tints[slot] = jnp.concatenate(
                [tone * (1.0 - tone) * sums, jnp.zeros((1, BLOCK), F32)], axis=0
            )


def backward_shapes(camera_ref, items_ref, shapes_rx, tints_rx, alphas, back, item_shapes):
    q0, q1, q2, q3 = (camera_ref[0, i] for i in range(4))
    place = lane_of((16, PIX))
    kind = level_of((16, PIX))
    at_x = ((place & (SIDE - 1)).astype(F32) - 7.5) / SIDE
    at_y = ((place >> 4).astype(F32) - 7.5) / SIDE
    basis = jnp.where(kind == 3, at_x * at_x + at_y * at_y, 0.0)
    basis = jnp.where(kind == 2, at_y, jnp.where(kind == 1, at_x, basis))
    basis = jnp.where(kind == 0, 1.0, basis).astype(BF16)
    along = ((1,), (1,))

    @pl.loop(0, TILES)
    def _(t):
        for k in range(DEPTH):
            e = items_ref[k, t]
            tile = item_rows(shapes_rx, e, GEO)
            slot = t * DEPTH + k
            rays = back[t, k]
            alpha = alphas[slot]
            ah, am, al = split(tinted(item_rows(tints_rx, e, TINT)))
            rh, rm, rl = split(rays)
            slope = product(
                stack([ah, ah, am, am, ah, al]), stack([rh, rm, rh, rm, rl, rh]), ((0,), (0,))
            )
            q = (slope - rays[4:5] / (1.0 - alpha)) * alpha
            moments = sum(product(basis, part, along) for part in split(q))
            m0, mx, my, mr = (moments[i : i + 1] for i in range(4))
            cu, cw = tile[0:1] - 0.5, tile[1:2] - 0.5
            twice = 2.0 * tile[2:3]
            du = twice * (mx - cu * m0)
            dw = twice * (my - cw * m0)
            spread = mr - 2.0 * (cu * mx + cw * my) + (cu * cu + cw * cw) * m0
            item_shapes[slot] = jnp.concatenate(
                [
                    (1.0 + q0) * du + q2 * dw,
                    q1 * du + (1.0 + q3) * dw,
                    twice * spread,
                    (1.0 - tile[3:4] / OPACITY_CAP) * m0,
                ],
                axis=0,
            )


def to_slots(items, place, out, count):
    parts = split(jnp.concatenate([items[i] for i in range(TILES * DEPTH)], axis=0))
    chunk = 256
    for part in range(NCELL * CAP * GEO // chunk):
        at = (level_of((chunk, TILES * DEPTH * GEO)) + part * chunk).astype(F32)
        spots = jnp.where(at == place, 1.0, 0.0).astype(BF16)
        found = sum(product(spots, x) for x in parts)
        for i in range(chunk // (CAP * GEO)):
            first, second = (found[(CAP * i + j) * GEO :][:count] for j in range(CAP))
            out[part * (chunk // (CAP * GEO)) + i] = jnp.concatenate([first, second], axis=0)


def step(
    camera_hbm, anchor_hbm, ids_hbm, items_hbm, goal_hbm, blur_hbm,
    params_hbm, first_hbm, second_hbm, out_ref, loss_ref,
    camera_ref, ids_ref, anchor_ref, items_ref, params_ref, first_ref, second_ref, ids_rows, items_rows, goal_ref, blur_ref,
    shapes, tints, shapes_tx, tints_tx, shapes_rx, tints_rx, alphas, firsts, seconds, merged, back,
    item_shapes, item_tints, shapes_back, tints_back, shapes_home, tints_home, summed, shares, rows, mine,
    stage_sem, early_send, late_send, shape_recv, tint_send, tint_recv,
    home_tint_send, home_tint_recv, home_send, home_recv, part_send, part_recv, row_send, row_recv,
):
    c = lax.axis_index("cell")
    v = lax.axis_index("view")
    z, y = lax.div(c, NY), lax.rem(c, NY)
    staged = [
        pltpu.make_async_copy(source, target, stage_sem.at[i])
        for i, (source, target) in enumerate(
            (
                (params_hbm, params_ref),
                (first_hbm, first_ref),
                (second_hbm, second_ref),
                (ids_hbm, ids_rows),
                (items_hbm, items_rows),
                (goal_hbm, goal_ref),
                (blur_hbm, blur_ref),
                (camera_hbm, camera_ref),
                (ids_hbm, ids_ref),
                (anchor_hbm, anchor_ref),
                (items_hbm, items_ref),
            )
        )
    ]
    for copy in staged:
        copy.start()

    barrier = pltpu.get_barrier_semaphore()

    @pl.loop(0, NCELL - 1, unroll=9)
    def _(i):
        pl.semaphore_signal(
            barrier, inc=1, device_id=(cell_peer(i, z, y), v), device_id_type=MESH
        )

    for i in range(1, NVIEW):
        pl.semaphore_signal(
            barrier, inc=1, device_id=(c, lax.rem(v + i, NVIEW)), device_id_type=MESH
        )

    for i in (0, 7, 8, 9, 10):
        staged[i].wait()
    derive(params_ref, camera_ref, shapes, tints)
    pl.semaphore_wait(barrier, NCELL - 1 + NVIEW - 1)

    def gather_shapes(o):
        row = level_of((GEO, BLOCK))
        shifts = [
            jnp.where(row == 0, anchor_ref[j, o], jnp.where(row == 1, anchor_ref[CAP + j, o], 0.0))
            for j in range(CAP)
        ]
        shapes_tx[o] = jnp.concatenate(
            [shapes[ids_ref[j, o] + 1] + shifts[j] for j in range(CAP)], axis=0
        )

    def gather_tints(o):
        tints_tx[o] = jnp.concatenate([tints[ids_ref[j, o] + 1] for j in range(CAP)], axis=0)

    def send(source, target, o, send_sem, recv_sem):
        pltpu.make_async_remote_copy(
            src_ref=source,
            dst_ref=target,
            send_sem=send_sem,
            recv_sem=recv_sem,
            device_id=(o, v),
            device_id_type=MESH,
        ).start()

    for low, high, sem in ((0, EARLY, early_send), (EARLY, NCELL - 1, late_send)):

        @pl.loop(low, high, unroll=3)
        def _(i):
            o = cell_peer(i, z, y)
            gather_shapes(o)
            send(shapes_tx.at[o], shapes_rx.at[c], o, sem, shape_recv)

    gather_shapes(c)
    pltpu.make_async_copy(shapes_tx.at[c], shapes_rx.at[c], shape_recv).start()

    for copy in staged[1:7]:
        copy.wait()
    goals = jnp.concatenate([goal_ref[ch] for ch in range(3)], axis=0)
    goal_blur = blurred(jnp.concatenate([goals, goals * goals], axis=0), blur_ref[...])
    ids = jnp.concatenate([ids_rows[0:1, :], ids_rows[1:2, :]], axis=1)
    chosen = jnp.where(level_of((NBLOCK, CAP * NCELL)) == ids, 1.0, 0.0).astype(BF16)
    own = row_of(v)
    row = jnp.minimum(own, COMP - 1)
    level = level_of((COMP, BLOCK))
    for b in range(NBLOCK):
        for i, ref in enumerate((params_ref, first_ref, second_ref)):
            only = jnp.where(level == row, ref[:, pl.ds(b * BLOCK, BLOCK)], 0.0)
            mine[i, pl.ds(b, 1), :] = jnp.sum(only, axis=0, keepdims=True)
    back[...] = jnp.zeros((TILES, DEPTH, GROUP, PIX), F32)
    merged[...] = jnp.zeros((5, DEPTH, TILES, PIX), F32)
    wide = (TILES, TILES * DEPTH * GEO)
    place = lax.rem(lane_of((1, wide[1])), GEO).astype(F32)
    for k in range(DEPTH):
        pick = jnp.where(lax.div(lane_of(wide), GEO) == level_of(wide) * DEPTH + k, 1.0, 0.0)
        entries = jnp.broadcast_to(items_rows[k : k + 1, :].astype(F32), (TILES, TILES))
        place = place + GEO * product(entries.astype(BF16), pick.astype(BF16))[0:1]

    def done(source, target, first, count, sem):
        span = pl.ds(first, count)
        pltpu.make_async_copy(source.at[span], target.at[span], sem).wait()

    done(shapes_tx, shapes_rx, 0, EARLY, early_send)

    @pl.loop(0, NCELL - 1, unroll=3)
    def _(i):
        o = cell_peer(i, z, y)
        gather_tints(o)
        send(tints_tx.at[o], tints_rx.at[c], o, tint_send, tint_recv)

    gather_tints(c)
    pltpu.make_async_copy(tints_tx.at[c], tints_rx.at[c], tint_recv).start()

    pltpu.make_async_copy(shapes_tx, shapes_rx, shape_recv).wait()
    cover(items_ref, shapes_rx, alphas, firsts, seconds, merged)
    pltpu.make_async_copy(tints_tx, tints_rx, tint_recv).wait()
    colour(items_ref, tints_rx, firsts, seconds, merged)
    compare(merged, goals, goal_blur, blur_ref, loss_ref, back)
    backward_tints(items_ref, tints_rx, firsts, seconds, back, item_tints)
    to_slots(item_tints, place, tints_back, TINT)

    @pl.loop(0, NCELL - 1, unroll=9)
    def _(i):
        o = cell_peer(i, z, y)
        send(tints_back.at[o], tints_home.at[c], o, home_tint_send, home_tint_recv)

    pltpu.make_async_copy(tints_back.at[c], tints_home.at[c], home_tint_recv).start()
    backward_shapes(camera_ref, items_ref, shapes_rx, tints_rx, alphas, back, item_shapes)
    to_slots(item_shapes, place, shapes_back, GEO)

    @pl.loop(0, NCELL - 1, unroll=9)
    def _(i):
        o = cell_peer(i, z, y)
        send(shapes_back.at[o], shapes_home.at[c], o, home_send, home_recv)

    pltpu.make_async_copy(shapes_back.at[c], shapes_home.at[c], home_recv).start()

    def part(i):
        w = lax.rem(v + i, NVIEW)
        return w, pltpu.make_async_remote_copy(
            src_ref=summed.at[jnp.minimum(row_of(w), COMP - 1)],
            dst_ref=shares.at[v],
            send_sem=part_send.at[i],
            recv_sem=part_recv.at[v],
            device_id=(c, w),
            device_id_type=MESH,
        )

    def arrived(buffer, sem, s):
        return pltpu.make_async_copy(buffer.at[s], buffer.at[s], sem.at[s])

    for source, target, sem, low, high in (
        (tints_back, tints_home, home_tint_recv, GEO, COMP),
        (shapes_back, shapes_home, home_recv, 0, GEO),
    ):
        pltpu.make_async_copy(source, target, sem).wait()
        for p in range(low, high):
            values = jnp.concatenate(
                [target[:, j * (high - low) + p - low, :] for j in range(CAP)], axis=0
            )
            summed[p] = sum(product(chosen, x) for x in split(values))
        for i in FAR_FIRST:
            w, copy = part(i)
            pl.when((row_of(w) >= low) & (row_of(w) < high))(copy.start)

    def send_row(i):
        return pltpu.make_async_remote_copy(
            src_ref=rows.at[row],
            dst_ref=rows.at[row],
            send_sem=row_send.at[i],
            recv_sem=row_recv.at[row],
            device_id=(c, lax.rem(v + i, NVIEW)),
            device_id_type=MESH,
        )

    @pl.when(v < COMP)
    def _():
        for s in range(NVIEW):
            pl.when(v != s)(arrived(shares, part_recv, s).wait)
        shares[v] = summed[row]
        grad = shares[0]
        for s in range(1, NVIEW):
            grad = grad + shares[s]
        one = BETA_ONE * mine[1] + (1.0 - BETA_ONE) * grad
        two = BETA_TWO * mine[2] + (1.0 - BETA_TWO) * grad * grad
        fix_one = 1.0 - BETA_ONE**FIRST_STEP
        fix_two = 1.0 - BETA_TWO**FIRST_STEP
        rows[row] = mine[0] - LEARN_RATE * (one / fix_one) / (jnp.sqrt(two / fix_two) + ADAM_EPS)
        for i in FAR_FIRST:
            send_row(i).start()

    for p in (*range(GEO, COMP), *range(GEO)):
        pl.when(own != p)(arrived(rows, row_recv, p).wait)
        for b in range(NBLOCK):
            out_ref[pl.ds(p, 1), pl.ds(b * BLOCK, BLOCK)] = rows[p, pl.ds(b, 1), :]

    done(shapes_tx, shapes_rx, 0, NCELL - 1 - EARLY, late_send)
    done(tints_tx, tints_rx, 0, NCELL - 1, tint_send)
    done(tints_back, tints_home, 0, NCELL - 1, home_tint_send)
    done(shapes_back, shapes_home, 0, NCELL - 1, home_send)
    for i in range(1, NVIEW):
        w, copy = part(i)
        pl.when(w < COMP)(copy.wait_send)

    @pl.when(v < COMP)
    def _():
        for i in range(1, NVIEW):
            send_row(i).wait_send()


def shards(
    params, first_moment, second_moment, camera, slot_block, slot_anchor, tile_items, target
):
    vmem = pl.BlockSpec(memory_space=pltpu.VMEM)
    hbm = pl.BlockSpec(memory_space=pltpu.HBM)
    ids = jnp.transpose(slot_block[0, 0, 0], (1, 0))
    anchors = jnp.transpose(slot_anchor[0, 0, 0], (0, 2, 1)).reshape(2 * CAP, NCELL)
    items = jnp.transpose(tile_items[0, 0], (1, 0))
    goals = jnp.transpose(target[0, 0], (1, 0, 2))
    whole = pltpu.VMEM((COMP, NBLOCK * BLOCK), F32)
    table = pltpu.VMEM((COMP, NBLOCK, BLOCK), F32)
    dma = pltpu.SemaphoreType.DMA
    new_params, losses = pl.pallas_call(
        step,
        out_shape=[
            jax.ShapeDtypeStruct((COMP, NBLOCK * BLOCK), F32),
            jax.ShapeDtypeStruct((1, 1, TILES), F32),
        ],
        in_specs=[hbm] * 9,
        out_specs=[vmem, vmem],
        scratch_shapes=[
            pltpu.SMEM((1, 4), F32),
            pltpu.SMEM((CAP, NCELL), jnp.int32),
            pltpu.SMEM((2 * CAP, NCELL), F32),
            pltpu.SMEM((DEPTH, TILES), jnp.int32),
            whole,
            whole,
            whole,
            pltpu.VMEM((CAP, NCELL), jnp.int32),
            pltpu.VMEM((DEPTH, TILES), jnp.int32),
            pltpu.VMEM((3, TILES, PIX), F32),
            pltpu.VMEM((PIX, PIX), F32),
            pltpu.VMEM((1 + NBLOCK, GEO, BLOCK), F32),
            pltpu.VMEM((1 + NBLOCK, TINT, BLOCK), F32),
            pltpu.VMEM((NCELL, CAP * GEO, BLOCK), F32),
            pltpu.VMEM((NCELL, CAP * TINT, BLOCK), F32),
            pltpu.VMEM((NCELL, CAP * GEO, BLOCK), F32),
            pltpu.VMEM((NCELL, CAP * TINT, BLOCK), F32),
            pltpu.VMEM((TILES * DEPTH, BLOCK, PIX), F32),
            pltpu.VMEM((TILES * DEPTH, BLOCK, PIX), BF16),
            pltpu.VMEM((TILES * DEPTH, BLOCK, PIX), BF16),
            pltpu.VMEM((5, DEPTH, TILES, PIX), F32),
            pltpu.VMEM((TILES, DEPTH, GROUP, PIX), F32),
            pltpu.VMEM((TILES * DEPTH, GEO, BLOCK), F32),
            pltpu.VMEM((TILES * DEPTH, GEO, BLOCK), F32),
            pltpu.VMEM((NCELL, CAP * GEO, BLOCK), F32),
            pltpu.VMEM((NCELL, CAP * TINT, BLOCK), F32),
            pltpu.VMEM((NCELL, CAP * GEO, BLOCK), F32),
            pltpu.VMEM((NCELL, CAP * TINT, BLOCK), F32),
            table,
            pltpu.VMEM((NVIEW, NBLOCK, BLOCK), F32),
            table,
            pltpu.VMEM((3, NBLOCK, BLOCK), F32),
            dma((11,)),
            *[dma] * 9,
            dma((NVIEW,)),
            dma((NVIEW,)),
            dma((NVIEW,)),
            dma((NVIEW,)),
        ],
        compiler_params=pltpu.CompilerParams(
            collective_id=0, has_side_effects=True, vmem_limit_bytes=56 << 20
        ),
    )(
        camera[0], anchors, ids, items, goals, blur_matrix(),
        params, first_moment, second_moment,
    )
    return (new_params, losses)


def solution(mesh):
    placed = (
        P(None, "cell"),
        P(None, "cell"),
        P(None, "cell"),
        P(None, "view", None),
        P(None, "view", "cell", None, None),
        P(None, "view", "cell", None, None, None),
        P(None, "view", "cell", None),
        P(None, "view", "cell", None, None),
    )
    return jax.shard_map(
        shards,
        mesh=mesh,
        in_specs=placed,
        out_specs=(P(None, "cell"), P(None, "view", "cell")),
        check_vma=False,
    )
```
